32 devices in a mesh: dp: 4 (over y, core), seq: 8 (over z, x).
Axes of the slice: x: 2, y: 2, z: 4, core: 2. Of those that a mesh axis runs over, the one named last changes fastest.
Arguments:
- queries: bfloat16 [4, 8192, 128], P('dp', 'seq'), may hold values from -6 to 6
- key_vectors: bfloat16 [4, 8192, 128], P('dp', 'seq'), may hold values from -6 to 6
- value_vectors: bfloat16 [4, 8192, 128], P('dp', 'seq'), may hold values from -6 to 6
- out_grad: bfloat16 [4, 8192, 128], P('dp', 'seq'), may hold values from -6 to 6
- log_decay: float32 [4, 1, 8192], P('dp', None, 'seq'), may hold values from -0.8 to 0, as said below
- prev_grads: bfloat16 [4, 256, 6144], P('dp', 'seq'), may hold values from -6 to 6
Outputs:
- attn_out: bfloat16 [4, 8192, 128], P('dp', 'seq')
- grad_query: bfloat16 [4, 8192, 128], P('dp', 'seq')
- grad_key: bfloat16 [4, 8192, 128], P('dp', 'seq')
- grad_value: bfloat16 [4, 8192, 128], P('dp', 'seq')
- grad_shard: float32 [256, 6144], P('seq', 'dp')
The draws below stay inside these ranges and needn't reach their ends.
Inputs may be any that keep to these rules, and one draw needn't show every extreme that they name: `log_decay`: every entry is negative.
All inputs are finite; a program needn't handle non-finite values.
Results may differ from the reference program's by a relative error of at most 0.012.
Values may be sent and summed in bfloat16 or wider, within the bound.
No kernel may reach another device: no remote copies, remote signals or barrier semaphores. Data moves between devices by JAX's collectives and lax.ppermute only.
A program may use at most 64 MiB of HBM per device.

```python
import math
import jax
import jax.numpy as jnp
from jax import lax

D = 6144
HEAD_DIM = 128
HEADS = 1
BLK = 512
TOK_DEV = 1024
SEQUENCE_TOKENS = 8192
GR_ROWS = 256
N_DP = 4


def draw_log_decay(key, part):
    random_key_array = jax.random.split(key, 7)
    flat_ids = jnp.arange(N_DP * HEADS).reshape(N_DP, HEADS)
    keeper_id = jax.random.randint(random_key_array[0], (), 0, N_DP * HEADS)
    coin_flags = jax.random.randint(random_key_array[1], (N_DP, HEADS), 0, 2) == 1
    fast_flags = coin_flags & (flat_ids != keeper_id)
    base_rate = jnp.where(fast_flags, 1.0 / 40.0, math.log(2.0) / SEQUENCE_TOKENS)[:, :, None]
    span_count = SEQUENCE_TOKENS // TOK_DEV
    span_scale = jnp.exp(jax.random.uniform(random_key_array[2], (N_DP, HEADS, span_count), minval=math.log(0.5), maxval=math.log(2.0)))
    span_scale = jnp.repeat(span_scale, TOK_DEV, axis=2)
    roughness = jax.random.uniform(random_key_array[3], (N_DP, HEADS, SEQUENCE_TOKENS), minval=0.5, maxval=1.5)
    decay_rates = -(base_rate * span_scale * roughness)
    first_spot = jax.random.randint(random_key_array[4], (N_DP,), 0, SEQUENCE_TOKENS)
    spot_gap = jax.random.randint(random_key_array[6], (N_DP,), 1, SEQUENCE_TOKENS)
    second_spot = (first_spot + spot_gap) % SEQUENCE_TOKENS
    spike_locations = jnp.stack([first_spot, second_spot], axis=1)
    spike_retained = jax.random.uniform(random_key_array[5], (N_DP, 2), minval=0.5, maxval=0.8)
    token_offsets = jnp.arange(SEQUENCE_TOKENS)[None, None, :]
    spike_matches = (token_offsets == spike_locations[:, :, None]).astype(jnp.float32)
    decay_spikes = jnp.sum(spike_matches * jnp.log(spike_retained)[:, :, None], axis=1)
    return (decay_rates + decay_spikes[:, None, :]).astype(jnp.float32)


def spiked(entries, stream_key, source, target, blocks, factor):
    owner, partner = [(jnp.arange(entries.shape[dim]) // (entries.shape[dim] // blocks)).reshape([-1 if axis == dim else 1 for axis in range(entries.ndim)]) for dim in (source, target)]
    chosen = jax.random.permutation(stream_key, blocks)[partner]
    strong = (owner == chosen) | (owner == (partner + blocks // 2) % blocks)
    return jnp.where(strong, factor * entries, entries)


def shard_levels(key, dims, shards, least, high):
    def one(dim, blocks):
        heights = jax.random.uniform(jax.random.fold_in(jax.random.fold_in(key, 6), dim), (blocks,), jnp.float32, least / len(shards), high / len(shards))
        return jnp.repeat(jnp.exp(heights), dims[dim] // blocks).reshape((-1,) + (1,) * (len(dims) - dim - 1))

    loudness = one(*shards[0])
    for cut in shards[1:]:
        loudness = loudness * one(*cut)
    return loudness


def centred(own_key, dims, width, limit, shards=(), kind=jnp.bfloat16):
    entries = width * jax.random.normal(own_key, dims, jnp.float32)
    if shards:
        entries = entries * shard_levels(own_key, dims, shards, -0.22, 0.18)
    return jnp.clip(entries, -limit, limit).astype(kind)


def noise_with(key, extent, scale, most, shards, heavy, kind=jnp.bfloat16):
    drawn = scale * jax.random.normal(key, extent, jnp.float32)
    if shards:
        drawn = drawn * shard_levels(key, extent, shards, -0.22, 0.18)
    return jnp.clip(spiked(drawn, jax.random.fold_in(key, 3), *heavy), -most, most).astype(kind)


def setup_inputs(seed: int = 0) -> dict:
    keys = jax.random.split(jax.random.key(seed), 7)
    queries = centred(keys[0], (N_DP, SEQUENCE_TOKENS, HEADS * HEAD_DIM), 1.0, 6.0, ((0, 4), (1, 8)))
    key_vectors = centred(keys[1], (N_DP, SEQUENCE_TOKENS, HEADS * HEAD_DIM), 1.0, 6.0, ((0, 4), (1, 8)))
    value_vectors = centred(keys[2], (N_DP, SEQUENCE_TOKENS, HEADS * HEAD_DIM), 1.0, 6.0, ((0, 4), (1, 8)))
    out_grad = centred(keys[3], (N_DP, SEQUENCE_TOKENS, HEADS * HEAD_DIM), 1.0, 6.0, ((0, 4), (1, 8)))
    log_decay = draw_log_decay(jax.random.fold_in(keys[6], 71), 0)
    prev_grads = noise_with(keys[5], (N_DP, GR_ROWS, D), 1.0, 6.0, ((0, 4), (1, 8)), (0, 2, 4, 2.0))
    return dict(queries=queries, key_vectors=key_vectors, value_vectors=value_vectors, out_grad=out_grad, log_decay=log_decay, prev_grads=prev_grads)


NORM_EPS = 1e-06
FULL_PRECISION = lax.Precision.HIGHEST

def product(left, right):
    return jnp.dot(left, right, precision=FULL_PRECISION, preferred_element_type=jnp.float32)

def decay_mask(running):
    spread = running[:, None] - running[None, :]
    lower_mask = jnp.tril(jnp.ones(spread.shape, dtype=bool))
    return jnp.where(lower_mask, jnp.exp(jnp.minimum(spread, 0.0)), 0.0)

def attend(query_rows, key_rows, value_rows, decay_rows):
    block_count = query_rows.shape[0] // BLK
    head_width = query_rows.shape[1]

    def advance(carried, block_inputs):
        query_block, key_block, value_block, decay_block = block_inputs
        running = jnp.cumsum(decay_block)
        scores = product(query_block, key_block.T) * decay_mask(running)
        block_out = product(scores, value_block) + jnp.exp(running)[:, None] * product(query_block, carried)
        weights = jnp.exp(running[-1] - running)
        updated = jnp.exp(running[-1]) * carried + product((key_block * weights[:, None]).T, value_block)
        return (updated, block_out)
    inputs = (query_rows.reshape(block_count, BLK, head_width), key_rows.reshape(block_count, BLK, head_width), value_rows.reshape(block_count, BLK, head_width), decay_rows.reshape(block_count, BLK))
    final_state, outputs = lax.scan(advance, jnp.zeros((head_width, head_width), jnp.float32), inputs)
    return outputs.reshape(block_count * BLK, head_width)

def reference(queries, key_vectors, value_vectors, out_grad, log_decay, prev_grads):
    head_count = log_decay.shape[1]

    def by_head(tensor):
        shaped = tensor.reshape(N_DP, SEQUENCE_TOKENS, head_count, HEAD_DIM).transpose(0, 2, 1, 3)
        return shaped.reshape(N_DP * head_count, SEQUENCE_TOKENS, HEAD_DIM).astype(jnp.float32)

    def to_rows(tensor):
        shaped = tensor.reshape(N_DP, head_count, SEQUENCE_TOKENS, HEAD_DIM).transpose(0, 2, 1, 3)
        return shaped.reshape(N_DP, SEQUENCE_TOKENS, head_count * HEAD_DIM).astype(jnp.bfloat16)
    items = (by_head(queries), by_head(key_vectors), by_head(value_vectors), by_head(out_grad), log_decay.reshape(N_DP * head_count, SEQUENCE_TOKENS))

    def per_item(item):
        query_rows, key_rows, value_rows, cotangent, decay_rows = item

        def forward(query_in, key_in, value_in):
            attention = attend(query_in, key_in, value_in, decay_rows)
            norm_ratio = lax.rsqrt(lax.optimization_barrier(jnp.mean(attention * attention, axis=-1, keepdims=True)) + NORM_EPS)
            return attention * norm_ratio
        normed, pullback = jax.vjp(forward, query_rows, key_rows, value_rows)
        grad_q, grad_k, grad_v = pullback(cotangent)
        return (normed, grad_q, grad_k, grad_v)
    normed, grad_q, grad_k, grad_v = lax.map(per_item, items)
    grad_shard = lax.optimization_barrier(jnp.sum(prev_grads.astype(jnp.float32), axis=0))
    return (to_rows(normed), to_rows(grad_q), to_rows(grad_k), to_rows(grad_v), grad_shard)
```

```python
import functools

import jax
import jax.numpy as jnp
from jax import lax
from jax.experimental import pallas as pl
from jax.experimental.pallas import tpu as pltpu
from jax.sharding import PartitionSpec as P

NORM_EPS = 1e-06
C = 128
F32 = jnp.float32
BF16 = jnp.bfloat16
LOGS = 16


def mm(a, b):
    return lax.dot_general(a, b, (((1,), (0,)), ((), ())), preferred_element_type=F32)


def mm_nt(a, b):
    return lax.dot_general(a, b, (((1,), (1,)), ((), ())), preferred_element_type=F32)


def split(x):
    high = x.astype(BF16)
    return high, (x - high.astype(F32)).astype(BF16)


def twice(x, axis):
    return jnp.concatenate([x, x], axis=axis)


def parts(x, axis):
    return jnp.concatenate(split(x), axis=axis)


def cut3(x):
    high = x.astype(BF16).astype(F32)
    middle = (x - high).astype(BF16).astype(F32)
    return high, middle, x - high - middle


def sums(decay):
    n = decay.shape[0]
    row = lax.broadcasted_iota(jnp.int32, (C, C), 0)
    col = lax.broadcasted_iota(jnp.int32, (C, C), 1)
    upto = (row <= col).astype(F32)
    after = (row > col).astype(F32)
    ones = jnp.concatenate([upto, after], axis=1).astype(BF16)
    pieces = jnp.concatenate(cut3(decay), axis=0).astype(BF16)
    both = mm(pieces, ones)
    both = both[:n] + both[n : 2 * n] + both[2 * n :]
    return both[:, :C], both[:, C:]


def totals(upto):
    n = upto.shape[0]
    return [jnp.broadcast_to(upto[r : r + 1, C - 1 :], (1, C)) for r in range(n)]


def before_chunks(tot):
    out = [jnp.zeros((1, C), F32)]
    for t in tot[:-1]:
        out.append(out[-1] + t)
    return out


def after_chunks(tot):
    return before_chunks(tot[::-1])[::-1]


def chunk(ref, r):
    return ref[r * C : (r + 1) * C, :]


def flipped(x):
    return x.astype(F32).T


def log_rows(total):
    high, middle, low = cut3(total)
    return jnp.concatenate([high, middle, low, jnp.zeros((LOGS - 3, C), F32)], axis=0).astype(BF16)


def read_log(ref):
    rows = ref[C:, :].astype(F32)
    return rows[0:1] + rows[1:2] + rows[2:3]


def state_kernel(k_ref, v_ref, decay_ref, out_ref):
    upto, after = sums(decay_ref[...])
    tot = totals(upto)
    later = after_chunks(tot)
    n = len(tot)
    state = jnp.zeros((C, C), F32)
    for r in range(n):
        weights = jnp.exp(after[r : r + 1] + later[r])
        kw = flipped(chunk(k_ref, r)) * weights
        state = state + mm(parts(kw, 1), twice(chunk(v_ref, r), 0))
    out_ref[:C, :] = state.astype(BF16)
    out_ref[C:, :] = log_rows(sum(tot))


def between(logs, positions, low, high):
    out = jnp.zeros((1, C), F32)
    for log, position in zip(logs, positions, strict=True):
        out = out + jnp.where((position > low) & (position < high), log, 0.0)
    return out


def place(stride, radix):
    return lax.rem(lax.div(lax.axis_index("seq"), stride), radix)


def fold_kernel(stride, radix, own_ref, *refs):
    out_ref = refs[-1]
    mine = place(stride, radix)
    positions = [mine ^ d for d in range(radix)]
    all_refs = [own_ref, *refs[:-1]]
    logs = [read_log(ref) for ref in all_refs]
    total = jnp.zeros((C, C), F32)
    for ref, position in zip(all_refs, positions, strict=True):
        weight = jnp.exp(between(logs, positions, position, radix))
        total = total + weight * ref[:C, :].astype(F32)
    out_ref[:C, :] = total.astype(BF16)
    out_ref[C:, :] = log_rows(sum(logs))


def forward_kernel(q_ref, k_ref, v_ref, decay_ref, order_ref, out_ref, cols_ref, qt_ref):
    upto, after = sums(decay_ref[...])
    tot = totals(upto)
    begin, later = before_chunks(tot), after_chunks(tot)
    n = len(tot)
    row = lax.broadcasted_iota(jnp.int32, (C, C), 0)
    col = lax.broadcasted_iota(jnp.int32, (C, C), 1)
    rows = [upto]
    rows.append(jnp.concatenate([jnp.exp(upto[r : r + 1] + begin[r]) for r in range(n)], axis=0))
    rows.append(jnp.concatenate([jnp.exp(after[r : r + 1] + later[r]) for r in range(n)], axis=0))
    rows.append(jnp.exp(upto))
    rows.append(jnp.exp(after))
    used = sum(x.shape[0] for x in rows)
    rows.append(jnp.zeros((C - used, C), F32))
    cols = jnp.concatenate(rows, axis=0).T
    cols_ref[...] = cols
    state = jnp.zeros((C, C), F32)
    for r in range(n):
        q, k, v = chunk(q_ref, r), chunk(k_ref, r), chunk(v_ref, r)
        decay = jnp.exp(jnp.minimum(cols[:, r : r + 1] - upto[r : r + 1], 0.0))
        scores = jnp.where(row >= col, mm_nt(q, k) * decay, 0.0)
        out = mm(parts(scores, 1), twice(v, 0))
        if r > 0:
            out = out + cols[:, 3 * n + r : 3 * n + r + 1] * mm(twice(q, 1), parts(state, 0))
        out_ref[r * C : (r + 1) * C, :] = out
        qt_ref[:, r * C : (r + 1) * C] = flipped(q).astype(BF16)
        if r < n - 1:
            kw = flipped(k) * jnp.exp(after[r : r + 1])
            state = jnp.exp(tot[r]) * state + mm(parts(kw, 1), twice(v, 0))


def norm_kernel(levels, count, local_ref, q_ref, qt_ref, dy_ref, cols_ref, *refs):
    received, (attn_ref, dattn_ref, incoming_ref, state_ref, weights_ref) = refs[:-5], refs[-5:]
    n = local_ref.shape[0] // C
    own, others = received[: len(levels)], received[len(levels) :]
    incoming = jnp.zeros((C, C), F32)
    ahead = jnp.zeros((1, C), F32)
    behind = jnp.zeros((1, C), F32)
    weights = []
    at = 0
    for (stride, radix), own_ref in zip(levels, own, strict=True):
        mine = place(stride, radix)
        positions = [mine ^ d for d in range(radix)]
        level = [own_ref, *others[at : at + radix - 1]]
        at += radix - 1
        logs = [read_log(ref) for ref in level]
        for ref, position in zip(level[1:], positions[1:], strict=True):
            weight = jnp.where(position < mine, jnp.exp(ahead + between(logs, positions, position, mine)), 0.0)
            incoming = incoming + weight * ref[:C, :].astype(F32)
            weights.append(
                jnp.where(position > mine, jnp.exp(behind + between(logs, positions, mine, position)), 0.0)
            )
        for position in positions:
            weights.append(jnp.exp(between(logs, positions, -1, position)))
        ahead = ahead + between(logs, positions, -1, mine)
        behind = behind + between(logs, positions, mine, radix)
    weights.append(jnp.zeros((count - len(weights), C), F32))
    weights_ref[...] = jnp.concatenate(weights, axis=0)
    incoming_ref[...] = incoming
    incoming = parts(incoming, 0)
    cols = cols_ref[...]
    state = jnp.zeros((C, C), F32)
    for r in range(n):
        lead = cols[:, n + r : n + r + 1]
        attention = chunk(local_ref, r) + lead * mm(twice(chunk(q_ref, r), 1), incoming)
        dy = chunk(dy_ref, r).astype(F32)
        ratio = lax.rsqrt(jnp.mean(attention * attention, axis=1, keepdims=True) + NORM_EPS)
        along = jnp.sum(dy * attention, axis=1, keepdims=True)
        attn_ref[r * C : (r + 1) * C, :] = (attention * ratio).astype(BF16)
        dattn = ratio * dy - (ratio * ratio * ratio / C * along) * attention
        dattn_ref[r * C : (r + 1) * C, :] = dattn
        both = mm(qt_ref[:, r * C : (r + 1) * C], parts(lead * dattn, 1))
        state = state + both[:, :C] + both[:, C:]
    state_ref[...] = state.astype(BF16)


def fold_back_kernel(first, own_ref, *refs):
    weights_ref, out_ref = refs[-2:]
    total = jnp.zeros((C, C), F32)
    for i, ref in enumerate((own_ref, *refs[:-2])):
        total = total + weights_ref[first + i : first + i + 1, :] * ref[...].astype(F32)
    out_ref[...] = total.astype(BF16)


def backward_kernel(
    q_ref, k_ref, v_ref, decay_ref, cols_ref, dattn_ref, incoming_ref, order_ref, dq_ref, dk_ref, dv_ref, starts
):
    upto, after = sums(decay_ref[...])
    tot = totals(upto)
    begin = before_chunks(tot)
    n = len(tot)
    row = lax.broadcasted_iota(jnp.int32, (C, C), 0)
    col = lax.broadcasted_iota(jnp.int32, (C, C), 1)
    cols = cols_ref[...]
    incoming = incoming_ref[...]
    state = jnp.zeros((C, C), F32)
    for r in range(n):
        starts[r] = state + jnp.exp(begin[r]) * incoming
        if r < n - 1:
            kw = flipped(chunk(k_ref, r)) * jnp.exp(after[r : r + 1])
            state = jnp.exp(tot[r]) * state + mm(parts(kw, 1), twice(chunk(v_ref, r), 0))
    future = jnp.zeros((C, C), F32)
    for r in reversed(range(n)):
        q, k, v = chunk(q_ref, r), chunk(k_ref, r), chunk(v_ref, r)
        dattn = chunk(dattn_ref, r)
        pair = parts(dattn, 1)
        up, down = upto[r : r + 1], cols[:, r : r + 1]
        lead, tail = cols[:, 3 * n + r : 3 * n + r + 1], cols[:, 4 * n + r : 4 * n + r + 1]
        lower = jnp.where(row >= col, jnp.exp(jnp.minimum(down - up, 0.0)), 0.0)
        upper = jnp.where(row <= col, jnp.exp(jnp.minimum(up - down, 0.0)), 0.0)
        v2 = twice(v, 1)
        dscores = mm_nt(pair, v2) * lower
        start = twice(starts[r].astype(BF16), 1)
        dq = mm(parts(dscores, 1), twice(k, 0)) + lead * mm_nt(pair, start)
        dq_ref[r * C : (r + 1) * C, :] = dq.astype(BF16)
        scores_t = mm_nt(k, q) * upper
        dscores_t = mm_nt(v2, pair) * upper
        high, low = split(dattn)
        s_high, s_low = split(scores_t)
        dk = mm(parts(dscores_t, 1), twice(q, 0))
        dv = mm(jnp.concatenate([s_high, s_low], 1), twice(high, 0)) + mm(s_high, low)
        if r < n - 1:
            dk = dk + tail * mm_nt(twice(v, 1), parts(future, 1))
            dv = dv + tail * mm(twice(k, 1), parts(future, 0))
        dk_ref[r * C : (r + 1) * C, :] = dk
        dv_ref[r * C : (r + 1) * C, :] = dv
        if r > 0:
            both = mm(flipped(q).astype(BF16), parts(lead * dattn, 1))
            future = jnp.exp(tot[r]) * future + both[:, :C] + both[:, C:]


def last_kernel(levels, dk_ref, dv_ref, k_ref, v_ref, cols_ref, weights_ref, *refs):
    received, (out_k_ref, out_v_ref) = refs[:-2], refs[-2:]
    n = dk_ref.shape[0] // C
    future = jnp.zeros((C, C), F32)
    at, taken = 0, 0
    for _, radix in levels:
        for d in range(radix - 1):
            future = future + weights_ref[at + d : at + d + 1, :] * received[taken + d][...].astype(F32)
        at += 2 * radix - 1
        taken += radix - 1
    cols = cols_ref[...]
    wide, tall = parts(future, 1), parts(future, 0)
    for r in range(n):
        tail = cols[:, 2 * n + r : 2 * n + r + 1]
        dk = chunk(dk_ref, r) + tail * mm_nt(twice(chunk(v_ref, r), 1), wide)
        dv = chunk(dv_ref, r) + tail * mm(twice(chunk(k_ref, r), 1), tall)
        out_k_ref[r * C : (r + 1) * C, :] = dk.astype(BF16)
        out_v_ref[r * C : (r + 1) * C, :] = dv.astype(BF16)


def call(body, shapes, name, scratch=(), flops=0, moved=1 << 20):
    return pl.pallas_call(
        body,
        out_shape=shapes,
        scratch_shapes=scratch,
        name=name,
        compiler_params=pltpu.CompilerParams(vmem_limit_bytes=32 * 1024 * 1024),
        cost_estimate=pl.CostEstimate(flops=flops, bytes_accessed=moved, transcendentals=0),
    )


def scan_levels(size):
    levels, stride = [], 1
    while stride < size:
        radix = 2 if stride == 1 else min(4, size // stride)
        levels.append((stride, radix))
        stride *= radix
    return levels


def swap(x, axis, size, stride, radix, d):
    pairs = [(i, i - i % (stride * radix) + ((i // stride % radix) ^ d) * stride + i % stride) for i in range(size)]
    return lax.ppermute(x, axis, pairs)


def local(levels, seq, dp, queries, key_vectors, value_vectors, out_grad, log_decay, prev_grads):
    q, k, v, dy = queries[0], key_vectors[0], value_vectors[0], out_grad[0]
    tokens = q.shape[0]
    n = tokens // C
    decay = log_decay.reshape(n, C)
    shape = jax.ShapeDtypeStruct
    payload = shape((C + LOGS, C), BF16)
    square = shape((C, C), F32)
    wide, narrow = shape((tokens, C), F32), shape((tokens, C), BF16)

    own = [call(state_kernel, payload, "state")(k, v, decay)]
    others = []
    for i, (stride, radix) in enumerate(levels):
        got = [swap(own[-1], "seq", seq, stride, radix, d) for d in range(1, radix)]
        others += got
        if i < len(levels) - 1:
            own.append(call(functools.partial(fold_kernel, stride, radix), payload, "fold")(own[-1], *got))
    local_out, cols, qt = call(forward_kernel, (wide, square, shape((C, tokens), BF16)), "forward")(
        q, k, v, decay, own[-1]
    )

    count = sum(2 * radix - 1 for _, radix in levels)
    count += -count % 8
    attn_out, dattn, incoming, state, weights = call(
        functools.partial(norm_kernel, levels, count),
        (narrow, wide, square, shape((C, C), BF16), shape((count, C), F32)),
        "norm",
    )(local_out, q, qt, dy, cols, *own, *others)

    received = []
    at = 0
    for i, (stride, radix) in enumerate(levels):
        got = [swap(state, "seq", seq, stride, radix, d) for d in range(1, radix)]
        received += got
        if i < len(levels) - 1:
            fold = functools.partial(fold_back_kernel, at + radix - 1)
            state = call(fold, shape((C, C), BF16), "fold_back")(state, *got, weights)
        at += 2 * radix - 1
    grad_query, dk, dv = call(
        backward_kernel, (narrow, wide, wide), "backward", scratch=[pltpu.VMEM((n, C, C), F32)]
    )(q, k, v, decay, cols, dattn, incoming, state)
    grad_key, grad_value = call(functools.partial(last_kernel, levels), (narrow, narrow), "last")(
        dk, dv, k, v, cols, weights, *received
    )

    mine = lax.axis_index("dp")
    grads = prev_grads[0]
    columns = grads.shape[1] // dp
    total = lax.dynamic_slice_in_dim(grads, mine * columns, columns, 1).astype(F32)
    for d in range(1, dp):
        away = lax.dynamic_slice_in_dim(grads, (mine ^ d) * columns, columns, 1)
        total = total + swap(away, "dp", dp, 1, dp, d).astype(F32)
    return attn_out[None], grad_query[None], grad_key[None], grad_value[None], total


def solution(mesh):
    seq, dp = mesh.shape["seq"], mesh.shape["dp"]
    return jax.shard_map(
        functools.partial(local, scan_levels(seq), seq, dp),
        mesh=mesh,
        in_specs=(
            P("dp", "seq", None),
            P("dp", "seq", None),
            P("dp", "seq", None),
            P("dp", "seq", None),
            P("dp", None, "seq"),
            P("dp", "seq", None),
        ),
        out_specs=(
            P("dp", "seq", None),
            P("dp", "seq", None),
            P("dp", "seq", None),
            P("dp", "seq", None),
            P("seq", "dp"),
        ),
        check_vma=False,
    )
```

```python
import functools

import jax
import jax.numpy as jnp
from jax import lax
from jax.experimental import pallas as pl
from jax.experimental.pallas import tpu as pltpu
from jax.sharding import PartitionSpec as P

NORM_EPS = 1e-06
C = 128
F32 = jnp.float32
BF16 = jnp.bfloat16
LOGS = 8


def mm(a, b):
    return lax.dot_general(a, b, (((1,), (0,)), ((), ())), preferred_element_type=F32)


def mm_nt(a, b):
    return lax.dot_general(a, b, (((1,), (1,)), ((), ())), preferred_element_type=F32)


def split(x):
    high = x.astype(BF16)
    return high, (x - high.astype(F32)).astype(BF16)


def twice(x, axis):
    return jnp.concatenate([x, x], axis=axis)


def parts(x, axis):
    return jnp.concatenate(split(x), axis=axis)


def cut3(x):
    high = x.astype(BF16).astype(F32)
    middle = (x - high).astype(BF16).astype(F32)
    return high, middle, x - high - middle


def sums(decay):
    n = decay.shape[0]
    row = lax.broadcasted_iota(jnp.int32, (C, C), 0)
    col = lax.broadcasted_iota(jnp.int32, (C, C), 1)
    upto = (row <= col).astype(F32)
    after = (row > col).astype(F32)
    ones = jnp.concatenate([upto, after], axis=1).astype(BF16)
    pieces = jnp.concatenate(cut3(decay), axis=0).astype(BF16)
    both = mm(pieces, ones)
    both = both[:n] + both[n : 2 * n] + both[2 * n :]
    return both[:, :C], both[:, C:]


def totals(upto):
    n = upto.shape[0]
    return [jnp.broadcast_to(upto[r : r + 1, C - 1 :], (1, C)) for r in range(n)]


def before_chunks(tot):
    out = [jnp.zeros((1, C), F32)]
    for t in tot[:-1]:
        out.append(out[-1] + t)
    return out


def after_chunks(tot):
    return before_chunks(tot[::-1])[::-1]


def chunk(ref, r):
    return ref[r * C : (r + 1) * C, :]


def flipped(x):
    return x.astype(F32).T


def log_rows(total):
    high, middle, low = cut3(total)
    return jnp.concatenate([high, middle, low, jnp.zeros((LOGS - 3, C), F32)], axis=0).astype(BF16)


def read_log(ref):
    rows = ref[C:, :].astype(F32)
    return rows[0:1] + rows[1:2] + rows[2:3]


def state_kernel(k_hbm, v_hbm, decay_hbm, out_ref, k_ref, v_ref, decay_ref, sems):
    pairs = ((decay_hbm, decay_ref), (k_hbm, k_ref), (v_hbm, v_ref))
    copies = [pltpu.make_async_copy(source, target, sems.at[i]) for i, (source, target) in enumerate(pairs)]
    for copy in copies:
        copy.start()
    copies[0].wait()
    upto, after = sums(decay_ref[...])
    tot = totals(upto)
    later = after_chunks(tot)
    weights = [jnp.exp(after[r : r + 1] + later[r]) for r in range(len(tot))]
    copies[1].wait()
    copies[2].wait()
    state = jnp.zeros((C, C), F32)
    for r, weight in enumerate(weights):
        kw = flipped(chunk(k_ref, r)) * weight
        state = state + mm(parts(kw, 1), twice(chunk(v_ref, r), 0))
    out_ref[:C, :] = state.astype(BF16)
    out_ref[C:, :] = log_rows(sum(tot))


def between(logs, positions, low, high):
    out = jnp.zeros((1, C), F32)
    for log, position in zip(logs, positions, strict=True):
        out = out + jnp.where((position > low) & (position < high), log, 0.0)
    return out


def place(stride, radix):
    return lax.rem(lax.div(lax.axis_index("seq"), stride), radix)


def fold_kernel(stride, radix, own_ref, *refs):
    out_ref = refs[-1]
    mine = place(stride, radix)
    positions = [mine ^ d for d in range(radix)]
    all_refs = [own_ref, *refs[: radix - 1]]
    logs = [read_log(ref) for ref in all_refs]
    total = jnp.zeros((C, C), F32)
    for ref, position in zip(all_refs, positions, strict=True):
        weight = jnp.exp(between(logs, positions, position, radix))
        total = total + weight * ref[:C, :].astype(F32)
    out_ref[:C, :] = total.astype(BF16)
    out_ref[C:, :] = log_rows(sum(logs))


def forward_kernel(
    q_ref, k_ref, v_ref, decay_ref, order_ref, out_ref, cols_ref, rows_ref, qt_ref, starts_ref, lower_ref
):
    upto, after = sums(decay_ref[...])
    tot = totals(upto)
    begin, later = before_chunks(tot), after_chunks(tot)
    n = len(tot)
    row = lax.broadcasted_iota(jnp.int32, (C, C), 0)
    col = lax.broadcasted_iota(jnp.int32, (C, C), 1)
    rows = [upto]
    rows.append(jnp.concatenate([jnp.exp(upto[r : r + 1] + begin[r]) for r in range(n)], axis=0))
    rows.append(jnp.concatenate([jnp.exp(after[r : r + 1] + later[r]) for r in range(n)], axis=0))
    rows.append(jnp.exp(upto))
    rows.append(jnp.exp(after))
    used = sum(x.shape[0] for x in rows)
    rows.append(jnp.zeros((C - used, C), F32))
    cols = jnp.concatenate(rows, axis=0).T
    cols_ref[...] = cols
    rows_ref[:n, :] = upto
    rows_ref[n : 2 * n, :] = jnp.concatenate([jnp.exp(x) for x in tot], axis=0)
    rows_ref[2 * n :, :] = jnp.concatenate([jnp.exp(x) for x in begin], axis=0)
    state = jnp.zeros((C, C), F32)
    for r in range(n):
        q, k, v = chunk(q_ref, r), chunk(k_ref, r), chunk(v_ref, r)
        decay = jnp.exp(jnp.minimum(cols[:, r : r + 1] - upto[r : r + 1], 0.0))
        lower = jnp.where(row >= col, decay, 0.0)
        lower_ref[r * C : (r + 1) * C, :] = lower
        scores = mm_nt(q, k) * lower
        out = mm(parts(scores, 1), twice(v, 0))
        if r > 0:
            out = out + cols[:, 3 * n + r : 3 * n + r + 1] * mm(twice(q, 1), parts(state, 0))
        out_ref[r * C : (r + 1) * C, :] = out
        qt_ref[:, r * C : (r + 1) * C] = flipped(q).astype(BF16)
        starts_ref[r * C : (r + 1) * C, :] = state
        if r < n - 1:
            kw = flipped(k) * jnp.exp(after[r : r + 1])
            state = jnp.exp(tot[r]) * state + mm(parts(kw, 1), twice(v, 0))


def turned_kernel(q_ref, k_ref, cols_ref, rows_ref, order_ref, scores_ref, upper_ref):
    n = rows_ref.shape[0] // 3
    row = lax.broadcasted_iota(jnp.int32, (C, C), 0)
    col = lax.broadcasted_iota(jnp.int32, (C, C), 1)
    cols = cols_ref[...]
    for r in range(n):
        decay = jnp.exp(jnp.minimum(rows_ref[r : r + 1, :] - cols[:, r : r + 1], 0.0))
        upper = jnp.where(row <= col, decay, 0.0)
        upper_ref[r * C : (r + 1) * C, :] = upper
        scores_ref[r * C : (r + 1) * C, :] = parts(mm_nt(chunk(k_ref, r), chunk(q_ref, r)) * upper, 1)


def norm_kernel(levels, count, local_ref, q_ref, qt_ref, dy_ref, cols_ref, *refs):
    received, (attn_ref, dattn_ref, incoming_ref, state_ref, weights_ref) = refs[:-5], refs[-5:]
    n = local_ref.shape[0] // C
    own, others = received[: len(levels)], received[len(levels) :]
    incoming = jnp.zeros((C, C), F32)
    ahead = jnp.zeros((1, C), F32)
    behind = jnp.zeros((1, C), F32)
    weights = []
    at = 0
    for (stride, radix), own_ref in zip(levels, own, strict=True):
        mine = place(stride, radix)
        positions = [mine ^ d for d in range(radix)]
        level = [own_ref, *others[at : at + radix - 1]]
        at += radix - 1
        logs = [read_log(ref) for ref in level]
        for ref, position in zip(level[1:], positions[1:], strict=True):
            weight = jnp.where(position < mine, jnp.exp(ahead + between(logs, positions, position, mine)), 0.0)
            incoming = incoming + weight * ref[:C, :].astype(F32)
            weights.append(
                jnp.where(position > mine, jnp.exp(behind + between(logs, positions, mine, position)), 0.0)
            )
        for position in positions:
            weights.append(jnp.exp(between(logs, positions, -1, position)))
        ahead = ahead + between(logs, positions, -1, mine)
        behind = behind + between(logs, positions, mine, radix)
    weights.append(jnp.zeros((count - len(weights), C), F32))
    weights_ref[...] = jnp.concatenate(weights, axis=0)
    incoming_ref[...] = incoming
    incoming = parts(incoming, 0)
    cols = cols_ref[...]
    state = jnp.zeros((C, C), F32)
    for r in range(n):
        lead = cols[:, n + r : n + r + 1]
        attention = chunk(local_ref, r) + lead * mm(twice(chunk(q_ref, r), 1), incoming)
        dy = chunk(dy_ref, r).astype(F32)
        ratio = lax.rsqrt(jnp.mean(attention * attention, axis=1, keepdims=True) + NORM_EPS)
        along = jnp.sum(dy * attention, axis=1, keepdims=True)
        attn_ref[r * C : (r + 1) * C, :] = (attention * ratio).astype(BF16)
        dattn = ratio * dy - (ratio * ratio * ratio / C * along) * attention
        dattn_ref[r * C : (r + 1) * C, :] = dattn
        both = mm(qt_ref[:, r * C : (r + 1) * C], parts(lead * dattn, 1))
        state = state + both[:, :C] + both[:, C:]
    state_ref[...] = state.astype(BF16)


def fold_back_kernel(first, radix, own_ref, *refs):
    weights_ref, out_ref = refs[radix - 1], refs[-1]
    total = jnp.zeros((C, C), F32)
    for i, ref in enumerate((own_ref, *refs[: radix - 1])):
        total = total + weights_ref[first + i : first + i + 1, :] * ref[...].astype(F32)
    out_ref[...] = total.astype(BF16)


def queries_kernel(
    columns, stride, k_ref, v_ref, cols_ref, rows_ref, starts_ref, lower_ref, dattn_ref, incoming_ref, order_ref, *refs
):
    attn_ref, have_ref, came_ref, attn_hbm, dq_hbm, total_hbm, done_ref, dq_ref, total_ref, sems = refs
    n = rows_ref.shape[0] // 3
    copies = [
        pltpu.make_async_copy(source, target, sems.at[i])
        for i, (source, target) in enumerate(((attn_ref, attn_hbm), (total_ref, total_hbm), (dq_ref, dq_hbm)))
    ]
    copies[0].start()
    total_ref[...] = half(have_ref, columns, bit(stride), 0).astype(F32) + came_ref[...].astype(F32)
    copies[1].start()
    cols = cols_ref[...]
    incoming = incoming_ref[...]
    for r in range(n):
        pair = parts(chunk(dattn_ref, r), 1)
        dscores = mm_nt(pair, twice(chunk(v_ref, r), 1)) * chunk(lower_ref, r)
        start = chunk(starts_ref, r) + rows_ref[2 * n + r : 2 * n + r + 1, :] * incoming
        dq = mm(parts(dscores, 1), twice(chunk(k_ref, r), 0))
        dq = dq + cols[:, 3 * n + r : 3 * n + r + 1] * mm_nt(pair, twice(start.astype(BF16), 1))
        dq_ref[r * C : (r + 1) * C, :] = dq.astype(BF16)
    copies[2].start()
    done_ref[...] = rows_ref[:n, :]
    for copy in copies:
        copy.wait()


def keys_kernel(
    q_ref, k_ref, v_ref, qt_ref, cols_ref, rows_ref, scores_ref, upper_ref, dattn_ref, order_ref, dk_ref, dv_ref
):
    n = rows_ref.shape[0] // 3
    cols = cols_ref[...]
    future = jnp.zeros((C, C), F32)
    for r in reversed(range(n)):
        k, v = chunk(k_ref, r), chunk(v_ref, r)
        dattn = chunk(dattn_ref, r)
        pair = parts(dattn, 1)
        lead, tail = cols[:, 3 * n + r : 3 * n + r + 1], cols[:, 4 * n + r : 4 * n + r + 1]
        dscores_t = mm_nt(twice(v, 1), pair) * chunk(upper_ref, r)
        scores = chunk(scores_ref, r)
        dk = mm(parts(dscores_t, 1), twice(chunk(q_ref, r), 0))
        dv = mm(scores, twice(pair[:, :C], 0)) + mm(scores[:, :C], pair[:, C:])
        if r < n - 1:
            dk = dk + tail * mm_nt(twice(v, 1), parts(future, 1))
            dv = dv + tail * mm(twice(k, 1), parts(future, 0))
        dk_ref[r * C : (r + 1) * C, :] = dk
        dv_ref[r * C : (r + 1) * C, :] = dv
        if r > 0:
            both = mm(qt_ref[:, r * C : (r + 1) * C], parts(lead * dattn, 1))
            future = rows_ref[n + r : n + r + 1, :] * future + both[:, :C] + both[:, C:]


def last_kernel(levels, dk_ref, dv_ref, k_ref, v_ref, cols_ref, weights_ref, *refs):
    received, (k_hbm, v_hbm, out_k_ref, out_v_ref, sems) = refs[:-5], refs[-5:]
    copies = [pltpu.make_async_copy(out_k_ref, k_hbm, sems.at[0]), pltpu.make_async_copy(out_v_ref, v_hbm, sems.at[1])]
    n = dk_ref.shape[0] // C
    future = jnp.zeros((C, C), F32)
    at, taken = 0, 0
    for _, radix in levels:
        for d in range(radix - 1):
            future = future + weights_ref[at + d : at + d + 1, :] * received[taken + d][...].astype(F32)
        at += 2 * radix - 1
        taken += radix - 1
    cols = cols_ref[...]
    wide, tall = parts(future, 1), parts(future, 0)
    for r in range(n):
        tail = cols[:, 2 * n + r : 2 * n + r + 1]
        dk = chunk(dk_ref, r) + tail * mm_nt(twice(chunk(v_ref, r), 1), wide)
        out_k_ref[r * C : (r + 1) * C, :] = dk.astype(BF16)
    copies[0].start()
    for r in range(n):
        tail = cols[:, 2 * n + r : 2 * n + r + 1]
        dv = chunk(dv_ref, r) + tail * mm(twice(chunk(k_ref, r), 1), tall)
        out_v_ref[r * C : (r + 1) * C, :] = dv.astype(BF16)
    copies[1].start()
    for copy in copies:
        copy.wait()


def half(ref, columns, odd, i):
    return ref[:, pl.ds(pl.multiple_of((2 * i + odd) * columns, C), columns)]


def bit(stride):
    return lax.rem(lax.div(lax.axis_index("dp"), stride), 2)


def cut_kernel(columns, have_ref, order_ref, sent_ref):
    for i in range(have_ref.shape[1] // columns // 2):
        sent_ref[:, i * columns : (i + 1) * columns] = half(have_ref, columns, 1 - bit(1), i)


def add_kernel(columns, stride, have_ref, came_ref, kept_ref, sent_ref):
    for i in range(have_ref.shape[1] // columns // 2):
        kept = half(have_ref, columns, bit(stride), i).astype(F32)
        kept_ref[:, i * columns : (i + 1) * columns] = kept + came_ref[:, i * columns : (i + 1) * columns].astype(F32)
    for i in range(kept_ref.shape[1] // columns // 2):
        sent_ref[:, i * columns : (i + 1) * columns] = half(kept_ref, columns, 1 - bit(2 * stride), i).astype(BF16)


def call(body, shapes, name, scratch=(), in_specs=None, out_specs=None, flops=0, moved=1024, vmem=32 << 20):
    specs = {}
    if in_specs is not None:
        specs["in_specs"] = in_specs
    if out_specs is not None:
        specs["out_specs"] = out_specs
    return pl.pallas_call(
        body,
        out_shape=shapes,
        scratch_shapes=scratch,
        name=name,
        compiler_params=pltpu.CompilerParams(vmem_limit_bytes=vmem),
        cost_estimate=pl.CostEstimate(flops=flops, bytes_accessed=moved, transcendentals=0),
        **specs,
    )


def scan_levels(size):
    levels, stride = [], 1
    while stride < size:
        radix = 2 if stride == 1 else min(4, size // stride)
        levels.append((stride, radix))
        stride *= radix
    return levels


def swap(x, axis, size, stride, radix, d):
    pairs = [(i, i - i % (stride * radix) + ((i // stride % radix) ^ d) * stride + i % stride) for i in range(size)]
    return lax.ppermute(x, axis, pairs)


def local(levels, seq, dp, queries, key_vectors, value_vectors, out_grad, log_decay, prev_grads):
    q, k, v, dy = queries[0], key_vectors[0], value_vectors[0], out_grad[0]
    tokens = q.shape[0]
    n = tokens // C
    decay = log_decay.reshape(n, C)
    shape = jax.ShapeDtypeStruct
    payload = shape((C + LOGS, C), BF16)
    square = shape((C, C), F32)
    wide, narrow = shape((tokens, C), F32), shape((tokens, C), BF16)

    away = pl.BlockSpec(memory_space=pltpu.HBM)
    here = pl.BlockSpec(memory_space=pltpu.VMEM)
    whole = pltpu.VMEM((tokens, C), BF16)
    dma = pltpu.SemaphoreType.DMA

    own = [
        call(
            state_kernel,
            payload,
            "state",
            scratch=[whole, whole, pltpu.VMEM((n, C), F32), dma((3,))],
            in_specs=[away] * 3,
        )(*[pltpu.with_memory_space_constraint(x, pltpu.HBM) for x in (k, v, decay)])
    ]
    grads = prev_grads[0]
    lines = grads.shape[0]
    columns = grads.shape[1] // dp
    others = []
    for i, (stride, radix) in enumerate(levels):
        got = [swap(own[-1], "seq", seq, stride, radix, d) for d in range(1, radix)]
        others += got
        if i == 0:
            sent = call(functools.partial(cut_kernel, columns), shape((lines, grads.shape[1] // 2), BF16), "cut")(grads, own[0])
            came = swap(sent, "dp", dp, 1, 2, 1)
            total, part = grads, 1
            while 2 * part < dp:
                kept, sent = shape((lines, total.shape[1] // 2), F32), shape((lines, total.shape[1] // 4), BF16)
                total, sent = call(functools.partial(add_kernel, columns, part), (kept, sent), "add")(total, came)
                part *= 2
                came = swap(sent, "dp", dp, part, 2, 1)
        if i < len(levels) - 1:
            fold = functools.partial(fold_kernel, stride, radix)
            own.append(call(fold, payload, "fold")(own[-1], *got, *([total] if i == 0 else [])))
    local_out, cols, rows, qt, starts, lower = call(
        forward_kernel, (wide, square, shape((3 * n, C), F32), shape((C, tokens), BF16), wide, wide), "forward"
    )(q, k, v, decay, own[-1])
    scores_t, upper = call(turned_kernel, (shape((tokens, 2 * C), BF16), wide), "turned")(q, k, cols, rows, own[-1])
    count = sum(2 * radix - 1 for _, radix in levels)
    count += -count % 8
    attention, dattn, incoming, state, weights = call(
        functools.partial(norm_kernel, levels, count),
        (narrow, wide, square, shape((C, C), BF16), shape((count, C), F32)),
        "norm",
    )(local_out, q, qt, dy, cols, *own, *others, scores_t)

    attn_out, grad_query, grad_shard, done = call(
        functools.partial(queries_kernel, columns, dp // 2),
        (narrow, narrow, shape((lines, columns), F32), shape((n, C), F32)),
        "queries",
        scratch=[whole, pltpu.VMEM((lines, columns), F32), dma((3,))],
        in_specs=[here] * 12,
        out_specs=(away, away, away, here),
    )(k, v, cols, rows, starts, lower, dattn, incoming, state, attention, total, came)
    received = []
    at = 0
    for i, (stride, radix) in enumerate(levels):
        got = [swap(state, "seq", seq, stride, radix, d) for d in range(1, radix)]
        received += got
        if i < len(levels) - 1:
            fold = functools.partial(fold_back_kernel, at + radix - 1, radix)
            state = call(fold, shape((C, C), BF16), "fold_back")(state, *got, weights, done)
        at += 2 * radix - 1
    dk, dv = call(keys_kernel, (wide, wide), "keys")(q, k, v, qt, cols, rows, scores_t, upper, dattn, state)
    grad_key, grad_value = call(
        functools.partial(last_kernel, levels),
        (narrow, narrow),
        "last",
        scratch=[whole, whole, dma((2,))],
        in_specs=[here] * (6 + len(received)),
        out_specs=(away, away),
    )(dk, dv, k, v, cols, weights, *received)
    return attn_out[None], grad_query[None], grad_key[None], grad_value[None], grad_shard


def solution(mesh):
    seq, dp = mesh.shape["seq"], mesh.shape["dp"]
    return jax.shard_map(
        functools.partial(local, scan_levels(seq), seq, dp),
        mesh=mesh,
        in_specs=(
            P("dp", "seq", None),
            P("dp", "seq", None),
            P("dp", "seq", None),
            P("dp", "seq", None),
            P("dp", None, "seq"),
            P("dp", "seq", None),
        ),
        out_specs=(
            P("dp", "seq", None),
            P("dp", "seq", None),
            P("dp", "seq", None),
            P("dp", "seq", None),
            P("seq", "dp"),
        ),
        check_vma=False,
    )
```

```python
import functools

import jax
import jax.numpy as jnp
from jax import lax
from jax.experimental import pallas as pl
from jax.experimental.pallas import tpu as pltpu
from jax.sharding import PartitionSpec as P

NORM_EPS = 1e-06
C = 128
F32 = jnp.float32
BF16 = jnp.bfloat16
FORWARD_OF_4 = ((2, 0, 3, 1), (3, 2, 1, 0), (1, 3, 0, 2))
LOGS = 8


def mm(a, b):
    return lax.dot_general(a, b, (((1,), (0,)), ((), ())), preferred_element_type=F32)


def mm_nt(a, b):
    return lax.dot_general(a, b, (((1,), (1,)), ((), ())), preferred_element_type=F32)


def split(x):
    high = x.astype(BF16)
    return high, (x - high.astype(F32)).astype(BF16)


def twice(x, axis):
    return jnp.concatenate([x, x], axis=axis)


def parts(x, axis):
    return jnp.concatenate(split(x), axis=axis)


def cut3(x):
    high = x.astype(BF16).astype(F32)
    middle = (x - high).astype(BF16).astype(F32)
    return high, middle, x - high - middle


def sums(decay):
    n = decay.shape[0]
    row = lax.broadcasted_iota(jnp.int32, (C, C), 0)
    col = lax.broadcasted_iota(jnp.int32, (C, C), 1)
    upto = (row <= col).astype(F32)
    after = (row > col).astype(F32)
    ones = jnp.concatenate([upto, after], axis=1).astype(BF16)
    pieces = jnp.concatenate(cut3(decay), axis=0).astype(BF16)
    both = mm(pieces, ones)
    both = both[:n] + both[n : 2 * n] + both[2 * n :]
    return both[:, :C], both[:, C:]


def totals(upto):
    n = upto.shape[0]
    return [jnp.broadcast_to(upto[r : r + 1, C - 1 :], (1, C)) for r in range(n)]


def before_chunks(tot):
    out = [jnp.zeros((1, C), F32)]
    for t in tot[:-1]:
        out.append(out[-1] + t)
    return out


def after_chunks(tot):
    return before_chunks(tot[::-1])[::-1]


def chunk(ref, r):
    return ref[r * C : (r + 1) * C, :]


def flipped(x):
    return x.astype(F32).T


def log_rows(total):
    high, middle, low = cut3(total)
    return jnp.concatenate([high, middle, low, jnp.zeros((LOGS - 3, C), F32)], axis=0).astype(BF16)


def read_log(ref):
    rows = ref[C:, :].astype(F32)
    return rows[0:1] + rows[1:2] + rows[2:3]


def state_kernel(k_hbm, v_hbm, decay_hbm, out_ref, k_ref, v_ref, decay_ref, sems):
    pairs = ((decay_hbm, decay_ref), (k_hbm, k_ref), (v_hbm, v_ref))
    copies = [pltpu.make_async_copy(source, target, sems.at[i]) for i, (source, target) in enumerate(pairs)]
    for copy in copies:
        copy.start()
    copies[0].wait()
    upto, after = sums(decay_ref[...])
    tot = totals(upto)
    later = after_chunks(tot)
    weights = [jnp.exp(after[r : r + 1] + later[r]) for r in range(len(tot))]
    copies[1].wait()
    copies[2].wait()
    state = jnp.zeros((C, C), F32)
    for r, weight in enumerate(weights):
        kw = flipped(chunk(k_ref, r)) * weight
        state = state + mm(parts(kw, 1), twice(chunk(v_ref, r), 0))
    out_ref[:C, :] = state.astype(BF16)
    out_ref[C:, :] = log_rows(sum(tot))


def between(logs, positions, low, high):
    out = jnp.zeros((1, C), F32)
    for log, position in zip(logs, positions, strict=True):
        out = out + jnp.where((position > low) & (position < high), log, 0.0)
    return out


def places(stride, radix, rounds):
    mine = lax.rem(lax.div(lax.axis_index("seq"), stride), radix)
    senders = [sum(jnp.where(mine == to, at, 0) for at, to in enumerate(targets)) for targets in rounds]
    return [mine, *senders]


def fold_kernel(stride, radix, rounds, own_ref, *refs):
    out_ref = refs[-1]
    positions = places(stride, radix, rounds)
    all_refs = [own_ref, *refs[: radix - 1]]
    logs = [read_log(ref) for ref in all_refs]
    total = jnp.zeros((C, C), F32)
    for ref, position in zip(all_refs, positions, strict=True):
        weight = jnp.exp(between(logs, positions, position, radix))
        total = total + weight * ref[:C, :].astype(F32)
    out_ref[:C, :] = total.astype(BF16)
    out_ref[C:, :] = log_rows(sum(logs))


def forward_kernel(
    q_ref, k_ref, v_ref, decay_ref, order_ref, dy_ref, out_ref, cols_ref, rows_ref, qt_ref, starts_ref, lower_ref, *wide_refs
):
    upto, after = sums(decay_ref[...])
    tot = totals(upto)
    begin, later = before_chunks(tot), after_chunks(tot)
    n = len(tot)
    row = lax.broadcasted_iota(jnp.int32, (C, C), 0)
    col = lax.broadcasted_iota(jnp.int32, (C, C), 1)
    rows = [upto]
    rows.append(jnp.concatenate([jnp.exp(upto[r : r + 1] + begin[r]) for r in range(n)], axis=0))
    rows.append(jnp.concatenate([jnp.exp(after[r : r + 1] + later[r]) for r in range(n)], axis=0))
    rows.append(jnp.exp(upto))
    rows.append(jnp.exp(after))
    used = sum(x.shape[0] for x in rows)
    rows.append(jnp.zeros((C - used, C), F32))
    cols = jnp.concatenate(rows, axis=0).T
    cols_ref[...] = cols
    rows_ref[:n, :] = upto
    rows_ref[n : 2 * n, :] = jnp.concatenate([jnp.exp(x) for x in tot], axis=0)
    rows_ref[2 * n :, :] = jnp.concatenate([jnp.exp(x) for x in begin], axis=0)
    state = jnp.zeros((C, C), F32)
    for r in range(n):
        q, k, v = chunk(q_ref, r), chunk(k_ref, r), chunk(v_ref, r)
        decay = jnp.exp(jnp.minimum(cols[:, r : r + 1] - upto[r : r + 1], 0.0))
        lower = jnp.where(row >= col, decay, 0.0)
        lower_ref[r * C : (r + 1) * C, :] = lower
        scores = mm_nt(q, k) * lower
        out = mm(parts(scores, 1), twice(v, 0))
        if r > 0:
            out = out + cols[:, 3 * n + r : 3 * n + r + 1] * mm(twice(q, 1), parts(state, 0))
        out_ref[r * C : (r + 1) * C, :] = out
        for i, ref in enumerate(wide_refs, 1):
            ref[r * C : (r + 1) * C, :] = jnp.broadcast_to(cols[:, i * n + r : i * n + r + 1], (C, C))
        qt_ref[:, r * C : (r + 1) * C] = flipped(q).astype(BF16)
        starts_ref[r * C : (r + 1) * C, :] = state
        if r < n - 1:
            kw = flipped(k) * jnp.exp(after[r : r + 1])
            state = jnp.exp(tot[r]) * state + mm(parts(kw, 1), twice(v, 0))


def turned_kernel(q_ref, k_ref, cols_ref, rows_ref, order_ref, scores_ref, upper_ref):
    n = rows_ref.shape[0] // 3
    row = lax.broadcasted_iota(jnp.int32, (C, C), 0)
    col = lax.broadcasted_iota(jnp.int32, (C, C), 1)
    cols = cols_ref[...]
    for r in range(n):
        decay = jnp.exp(jnp.minimum(rows_ref[r : r + 1, :] - cols[:, r : r + 1], 0.0))
        upper = jnp.where(row <= col, decay, 0.0)
        upper_ref[r * C : (r + 1) * C, :] = upper
        scores_ref[r * C : (r + 1) * C, :] = parts(mm_nt(chunk(k_ref, r), chunk(q_ref, r)) * upper, 1)


def norm_kernel(levels, count, local_ref, q_ref, qt_ref, dy_ref, lead_ref, *refs):
    received, (attn_ref, dattn_ref, incoming_ref, state_ref, weights_ref) = refs[:-5], refs[-5:]
    n = local_ref.shape[0] // C
    own, others = received[: len(levels)], received[len(levels) :]
    incoming = jnp.zeros((C, C), F32)
    ahead = jnp.zeros((1, C), F32)
    behind = jnp.zeros((1, C), F32)
    weights = []
    at = 0
    for (stride, radix, rounds, back_rounds), own_ref in zip(levels, own, strict=True):
        positions = places(stride, radix, rounds)
        mine = positions[0]
        level = [own_ref, *others[at : at + radix - 1]]
        at += radix - 1
        logs = [read_log(ref) for ref in level]
        for ref, position in zip(level[1:], positions[1:], strict=True):
            weight = jnp.where(position < mine, jnp.exp(ahead + between(logs, positions, position, mine)), 0.0)
            incoming = incoming + weight * ref[:C, :].astype(F32)
        senders = places(stride, radix, back_rounds)
        for position in senders[1:]:
            weights.append(
                jnp.where(position > mine, jnp.exp(behind + between(logs, positions, mine, position)), 0.0)
            )
        for position in senders:
            weights.append(jnp.exp(between(logs, positions, -1, position)))
        ahead = ahead + between(logs, positions, -1, mine)
        behind = behind + between(logs, positions, mine, radix)
    weights.append(jnp.zeros((count - len(weights), C), F32))
    weights_ref[...] = jnp.concatenate(weights, axis=0)
    incoming_ref[...] = incoming
    incoming = parts(incoming, 0)
    state = jnp.zeros((C, C), F32)
    for r in range(n):
        lead = chunk(lead_ref, r)
        attention = chunk(local_ref, r) + lead * mm(twice(chunk(q_ref, r), 1), incoming)
        dy = chunk(dy_ref, r).astype(F32)
        ratio = lax.rsqrt(jnp.mean(attention * attention, axis=1, keepdims=True) + NORM_EPS)
        along = jnp.sum(dy * attention, axis=1, keepdims=True)
        attn_ref[r * C : (r + 1) * C, :] = (attention * ratio).astype(BF16)
        dattn = ratio * dy - (ratio * ratio * ratio / C * along) * attention
        dattn_ref[r * C : (r + 1) * C, :] = dattn
        both = mm(qt_ref[:, r * C : (r + 1) * C], parts(lead * dattn, 1))
        state = state + both[:, :C] + both[:, C:]
    state_ref[...] = state.astype(BF16)


def fold_back_kernel(first, radix, own_ref, *refs):
    weights_ref, out_ref = refs[radix - 1], refs[-1]
    total = jnp.zeros((C, C), F32)
    for i, ref in enumerate((own_ref, *refs[: radix - 1])):
        total = total + weights_ref[first + i : first + i + 1, :] * ref[...].astype(F32)
    out_ref[...] = total.astype(BF16)


def queries_kernel(
    columns, stride, k_ref, v_ref, cols_ref, rows_ref, starts_ref, lower_ref, dattn_ref, incoming_ref, order_ref, *refs
):
    attn_ref, have_ref, came_ref, attn_hbm, dq_hbm, total_hbm, done_ref, dq_ref, total_ref, sems = refs
    n = rows_ref.shape[0] // 3
    copies = [
        pltpu.make_async_copy(source, target, sems.at[i])
        for i, (source, target) in enumerate(((attn_ref, attn_hbm), (total_ref, total_hbm), (dq_ref, dq_hbm)))
    ]
    copies[0].start()
    total_ref[...] = half(have_ref, columns, bit(stride), 0).astype(F32) + came_ref[...].astype(F32)
    copies[1].start()
    cols = cols_ref[...]
    incoming = incoming_ref[...]
    for r in range(n):
        pair = parts(chunk(dattn_ref, r), 1)
        dscores = mm_nt(pair, twice(chunk(v_ref, r), 1)) * chunk(lower_ref, r)
        start = chunk(starts_ref, r) + rows_ref[2 * n + r : 2 * n + r + 1, :] * incoming
        dq = mm(parts(dscores, 1), twice(chunk(k_ref, r), 0))
        dq = dq + cols[:, 3 * n + r : 3 * n + r + 1] * mm_nt(pair, twice(start.astype(BF16), 1))
        dq_ref[r * C : (r + 1) * C, :] = dq.astype(BF16)
    copies[2].start()
    done_ref[...] = rows_ref[:n, :]
    for copy in copies:
        copy.wait()


def keys_kernel(
    q_ref, k_ref, v_ref, qt_ref, cols_ref, rows_ref, scores_ref, upper_ref, dattn_ref, order_ref, dk_ref, dv_ref
):
    n = rows_ref.shape[0] // 3
    cols = cols_ref[...]
    future = jnp.zeros((C, C), F32)
    for r in reversed(range(n)):
        k, v = chunk(k_ref, r), chunk(v_ref, r)
        dattn = chunk(dattn_ref, r)
        pair = parts(dattn, 1)
        lead, tail = cols[:, 3 * n + r : 3 * n + r + 1], cols[:, 4 * n + r : 4 * n + r + 1]
        dscores_t = mm_nt(twice(v, 1), pair) * chunk(upper_ref, r)
        scores = chunk(scores_ref, r)
        dk = mm(parts(dscores_t, 1), twice(chunk(q_ref, r), 0))
        dv = mm(scores, twice(pair[:, :C], 0)) + mm(scores[:, :C], pair[:, C:])
        if r < n - 1:
            dk = dk + tail * mm_nt(twice(v, 1), parts(future, 1))
            dv = dv + tail * mm(twice(k, 1), parts(future, 0))
        dk_ref[r * C : (r + 1) * C, :] = dk
        dv_ref[r * C : (r + 1) * C, :] = dv
        if r > 0:
            both = mm(qt_ref[:, r * C : (r + 1) * C], parts(lead * dattn, 1))
            future = rows_ref[n + r : n + r + 1, :] * future + both[:, :C] + both[:, C:]


def last_kernel(levels, dk_ref, dv_ref, k_ref, v_ref, tail_ref, weights_ref, *refs):
    received, (k_hbm, v_hbm, out_k_ref, out_v_ref, sems) = refs[:-5], refs[-5:]
    n = dk_ref.shape[0] // C
    future = jnp.zeros((C, C), F32)
    at, taken = 0, 0
    for _, radix, _, _ in levels:
        for d in range(radix - 1):
            future = future + weights_ref[at + d : at + d + 1, :] * received[taken + d][...].astype(F32)
        at += 2 * radix - 1
        taken += radix - 1
    wide, tall = parts(future, 1), parts(future, 0)
    copies = []
    for r in range(n):
        tail = chunk(tail_ref, r)
        dk = chunk(dk_ref, r) + tail * mm_nt(twice(chunk(v_ref, r), 1), wide)
        out_k_ref[r * C : (r + 1) * C, :] = dk.astype(BF16)
        dv = chunk(dv_ref, r) + tail * mm(twice(chunk(k_ref, r), 1), tall)
        out_v_ref[r * C : (r + 1) * C, :] = dv.astype(BF16)
        if (r + 1) % (n // 2) == 0:
            rows = pl.ds((r + 1 - n // 2) * C, n // 2 * C)
            for source, target in ((out_k_ref, k_hbm), (out_v_ref, v_hbm)):
                copies.append(pltpu.make_async_copy(source.at[rows], target.at[rows], sems.at[len(copies)]))
                copies[-1].start()
    for copy in copies:
        copy.wait()


def half(ref, columns, odd, i):
    return ref[:, pl.ds(pl.multiple_of((2 * i + odd) * columns, C), columns)]


def bit(stride):
    return lax.rem(lax.div(lax.axis_index("dp"), stride), 2)


def cut_kernel(columns, have_ref, order_ref, sent_ref):
    for i in range(have_ref.shape[1] // columns // 2):
        sent_ref[:, i * columns : (i + 1) * columns] = half(have_ref, columns, 1 - bit(1), i)


def add_kernel(columns, stride, have_ref, came_ref, kept_ref, sent_ref):
    for i in range(have_ref.shape[1] // columns // 2):
        kept = half(have_ref, columns, bit(stride), i).astype(F32)
        kept_ref[:, i * columns : (i + 1) * columns] = kept + came_ref[:, i * columns : (i + 1) * columns].astype(F32)
    for i in range(kept_ref.shape[1] // columns // 2):
        sent_ref[:, i * columns : (i + 1) * columns] = half(kept_ref, columns, 1 - bit(2 * stride), i).astype(BF16)


def call(body, shapes, name, scratch=(), in_specs=None, out_specs=None, flops=0, moved=1024, vmem=32 << 20):
    specs = {}
    if in_specs is not None:
        specs["in_specs"] = in_specs
    if out_specs is not None:
        specs["out_specs"] = out_specs
    return pl.pallas_call(
        body,
        out_shape=shapes,
        scratch_shapes=scratch,
        name=name,
        compiler_params=pltpu.CompilerParams(vmem_limit_bytes=vmem),
        cost_estimate=pl.CostEstimate(flops=flops, bytes_accessed=moved, transcendentals=0),
        **specs,
    )


def exchanges(radix):
    return tuple(tuple(at ^ d for at in range(radix)) for d in range(1, radix))


def scan_levels(size):
    levels, stride = [], 1
    while stride < size:
        radix = 2 if stride == 1 else min(4, size // stride)
        pairs = exchanges(radix)
        levels.append((stride, radix, FORWARD_OF_4 if radix == 4 else pairs, pairs))
        stride *= radix
    return levels


def send(x, axis, size, stride, targets):
    radix = len(targets)
    pairs = [(i, i + (targets[i // stride % radix] - i // stride % radix) * stride) for i in range(size)]
    return lax.ppermute(x, axis, pairs)


def local(levels, seq, dp, queries, key_vectors, value_vectors, out_grad, log_decay, prev_grads):
    q, k, v, dy = queries[0], key_vectors[0], value_vectors[0], out_grad[0]
    tokens = q.shape[0]
    n = tokens // C
    decay = log_decay.reshape(n, C)
    shape = jax.ShapeDtypeStruct
    payload = shape((C + LOGS, C), BF16)
    square = shape((C, C), F32)
    wide, narrow = shape((tokens, C), F32), shape((tokens, C), BF16)

    away = pl.BlockSpec(memory_space=pltpu.HBM)
    here = pl.BlockSpec(memory_space=pltpu.VMEM)
    whole = pltpu.VMEM((tokens, C), BF16)
    dma = pltpu.SemaphoreType.DMA

    own = [
        call(
            state_kernel,
            payload,
            "state",
            scratch=[whole, whole, pltpu.VMEM((n, C), F32), dma((3,))],
            in_specs=[away] * 3,
        )(*[pltpu.with_memory_space_constraint(x, pltpu.HBM) for x in (k, v, decay)])
    ]
    grads = prev_grads[0]
    lines = grads.shape[0]
    columns = grads.shape[1] // dp
    others = []
    for i, (stride, radix, rounds, _) in enumerate(levels):
        got = [send(own[-1], "seq", seq, stride, targets) for targets in rounds]
        others += got
        if i == 0:
            sent = call(functools.partial(cut_kernel, columns), shape((lines, grads.shape[1] // 2), BF16), "cut")(grads, own[0])
            came = send(sent, "dp", dp, 1, (1, 0))
            total, part = grads, 1
            while 2 * part < dp:
                kept, sent = shape((lines, total.shape[1] // 2), F32), shape((lines, total.shape[1] // 4), BF16)
                total, sent = call(functools.partial(add_kernel, columns, part), (kept, sent), "add")(total, came)
                part *= 2
                came = send(sent, "dp", dp, part, (1, 0))
        if i < len(levels) - 1:
            fold = functools.partial(fold_kernel, stride, radix, rounds)
            own.append(call(fold, payload, "fold")(own[-1], *got, *([total] if i == 0 else [])))
    local_out, cols, rows, qt, starts, lower, lead, tail = call(
        forward_kernel, (wide, square, shape((3 * n, C), F32), shape((C, tokens), BF16), wide, wide, wide, wide), "forward"
    )(q, k, v, decay, own[-1], dy)
    scores_t, upper = call(turned_kernel, (shape((tokens, 2 * C), BF16), wide), "turned")(q, k, cols, rows, own[-1])
    count = sum(2 * radix - 1 for _, radix, _, _ in levels)
    count += -count % 8
    attention, dattn, incoming, state, weights = call(
        functools.partial(norm_kernel, levels, count),
        (narrow, wide, square, shape((C, C), BF16), shape((count, C), F32)),
        "norm",
    )(local_out, q, qt, dy, lead, *own, *others, scores_t)

    attn_out, grad_query, grad_shard, done = call(
        functools.partial(queries_kernel, columns, dp // 2),
        (narrow, narrow, shape((lines, columns), F32), shape((n, C), F32)),
        "queries",
        scratch=[whole, pltpu.VMEM((lines, columns), F32), dma((3,))],
        in_specs=[here] * 12,
        out_specs=(away, away, away, here),
    )(k, v, cols, rows, starts, lower, dattn, incoming, state, attention, total, came)
    received = []
    at = 0
    for i, (stride, radix, _, rounds) in enumerate(levels):
        got = [send(state, "seq", seq, stride, targets) for targets in rounds]
        received += got
        if i < len(levels) - 1:
            fold = functools.partial(fold_back_kernel, at + radix - 1, radix)
            state = call(fold, shape((C, C), BF16), "fold_back")(state, *got, weights, done)
        at += 2 * radix - 1
    dk, dv = call(keys_kernel, (wide, wide), "keys")(q, k, v, qt, cols, rows, scores_t, upper, dattn, state)
    grad_key, grad_value = call(
        functools.partial(last_kernel, levels),
        (narrow, narrow),
        "last",
        scratch=[whole, whole, dma((4,))],
        in_specs=[here] * (6 + len(received)),
        out_specs=(away, away),
    )(dk, dv, k, v, tail, weights, *received)
    return attn_out[None], grad_query[None], grad_key[None], grad_value[None], grad_shard


def solution(mesh):
    seq, dp = mesh.shape["seq"], mesh.shape["dp"]
    return jax.shard_map(
        functools.partial(local, scan_levels(seq), seq, dp),
        mesh=mesh,
        in_specs=(
            P("dp", "seq", None),
            P("dp", "seq", None),
            P("dp", "seq", None),
            P("dp", "seq", None),
            P("dp", None, "seq"),
            P("dp", "seq", None),
        ),
        out_specs=(
            P("dp", "seq", None),
            P("dp", "seq", None),
            P("dp", "seq", None),
            P("dp", "seq", None),
            P("seq", "dp"),
        ),
        check_vma=False,
    )
```

```python
import functools

import jax
import jax.numpy as jnp
from jax import lax
from jax.experimental import pallas as pl
from jax.experimental.pallas import tpu as pltpu
from jax.sharding import PartitionSpec as P

NORM_EPS = 1e-06
C = 128
F32 = jnp.float32
BF16 = jnp.bfloat16
FORWARD_OF_4 = ((3, 0, 1, 2), (2, 3, 0, 1), (1, 2, 3, 0))
LAST_BACKWARD_OF_4 = ((1, 0, 3, 2), (2, 3, 0, 1), (2, 3, 1, 0))
LOGS = 8


def mm(a, b):
    return lax.dot_general(a, b, (((1,), (0,)), ((), ())), preferred_element_type=F32)


def mm_nt(a, b):
    return lax.dot_general(a, b, (((1,), (1,)), ((), ())), preferred_element_type=F32)


def split(x):
    high = x.astype(BF16)
    return high, (x - high.astype(F32)).astype(BF16)


def twice(x, axis):
    return jnp.concatenate([x, x], axis=axis)


def parts(x, axis):
    return jnp.concatenate(split(x), axis=axis)


def cut3(x):
    high = x.astype(BF16).astype(F32)
    middle = (x - high).astype(BF16).astype(F32)
    return high, middle, x - high - middle


def sums(decay):
    n = decay.shape[0]
    row = lax.broadcasted_iota(jnp.int32, (C, C), 0)
    col = lax.broadcasted_iota(jnp.int32, (C, C), 1)
    upto = (row <= col).astype(F32)
    after = (row > col).astype(F32)
    ones = jnp.concatenate([upto, after], axis=1).astype(BF16)
    pieces = jnp.concatenate(cut3(decay), axis=0).astype(BF16)
    both = mm(pieces, ones)
    both = both[:n] + both[n : 2 * n] + both[2 * n :]
    return both[:, :C], both[:, C:]


def totals(upto):
    n = upto.shape[0]
    return [jnp.broadcast_to(upto[r : r + 1, C - 1 :], (1, C)) for r in range(n)]


def before_chunks(tot):
    out = [jnp.zeros((1, C), F32)]
    for t in tot[:-1]:
        out.append(out[-1] + t)
    return out


def after_chunks(tot):
    return before_chunks(tot[::-1])[::-1]


def chunk(ref, r):
    return ref[r * C : (r + 1) * C, :]


def flipped(x):
    return x.astype(F32).T


def log_rows(total):
    high, middle, low = cut3(total)
    return jnp.concatenate([high, middle, low, jnp.zeros((LOGS - 3, C), F32)], axis=0).astype(BF16)


def read_log(ref):
    rows = ref[C:, :].astype(F32)
    return rows[0:1] + rows[1:2] + rows[2:3]


def state_kernel(k_hbm, v_hbm, decay_hbm, out_ref, k_ref, v_ref, decay_ref, sems):
    pairs = ((decay_hbm, decay_ref), (k_hbm, k_ref), (v_hbm, v_ref))
    copies = [pltpu.make_async_copy(source, target, sems.at[i]) for i, (source, target) in enumerate(pairs)]
    for copy in copies:
        copy.start()
    copies[0].wait()
    upto, after = sums(decay_ref[...])
    tot = totals(upto)
    later = after_chunks(tot)
    weights = [jnp.exp(after[r : r + 1] + later[r]) for r in range(len(tot))]
    copies[1].wait()
    copies[2].wait()
    state = jnp.zeros((C, C), F32)
    for r, weight in enumerate(weights):
        kw = flipped(chunk(k_ref, r)) * weight
        state = state + mm(kw.astype(BF16), chunk(v_ref, r))
    out_ref[:C, :] = state.astype(BF16)
    out_ref[C:, :] = log_rows(sum(tot))


def between(logs, positions, low, high):
    out = jnp.zeros((1, C), F32)
    for log, position in zip(logs, positions, strict=True):
        out = out + jnp.where((position > low) & (position < high), log, 0.0)
    return out


def places(stride, radix, rounds):
    block = lax.rem(lax.axis_index("seq"), stride * radix)
    senders = [sum(jnp.where(block == to, at // stride, 0) for at, to in enumerate(targets)) for targets in rounds]
    return [lax.div(block, stride), *senders]


def fold_kernel(stride, radix, rounds, own_ref, *refs):
    out_ref = refs[-1]
    positions = places(stride, radix, rounds)
    all_refs = [own_ref, *refs[: radix - 1]]
    logs = [read_log(ref) for ref in all_refs]
    total = jnp.zeros((C, C), F32)
    for ref, position in zip(all_refs, positions, strict=True):
        weight = jnp.exp(between(logs, positions, position, radix))
        total = total + weight * ref[:C, :].astype(F32)
    out_ref[:C, :] = total.astype(BF16)
    out_ref[C:, :] = log_rows(sum(logs))


def spread(decay_row):
    row = lax.broadcasted_iota(jnp.int32, (C, C), 0)
    col = lax.broadcasted_iota(jnp.int32, (C, C), 1)
    pieces = jnp.concatenate([jnp.where(row >= col, x, 0.0) for x in cut3(decay_row)], axis=1).astype(BF16)
    return mm(pieces, jnp.ones((3 * C, C), BF16))


def forward_kernel(
    q_ref, k_ref, v_ref, decay_ref, order_ref, dy_ref, out_ref, downs_ref, rows_ref, qt_ref, starts_ref, lower_ref, lead_ref
):
    upto, after = sums(decay_ref[...])
    tot = totals(upto)
    begin, later = before_chunks(tot), after_chunks(tot)
    n = len(tot)
    row = lax.broadcasted_iota(jnp.int32, (C, C), 0)
    col = lax.broadcasted_iota(jnp.int32, (C, C), 1)
    rows_ref[:n, :] = upto
    for i, rows in enumerate(([jnp.exp(x) for x in tot], [jnp.exp(x) for x in begin], tot, later), 1):
        rows_ref[i * n : (i + 1) * n, :] = jnp.concatenate(rows, axis=0)
    state = jnp.zeros((C, C), F32)
    for r in range(n):
        q, k, v = chunk(q_ref, r), chunk(k_ref, r), chunk(v_ref, r)
        down = spread(decay_ref[r : r + 1, :])
        downs_ref[r * C : (r + 1) * C, :] = down
        lead_ref[r * C : (r + 1) * C, :] = jnp.exp(down + begin[r])
        lower = jnp.where(row >= col, jnp.exp(jnp.minimum(down - upto[r : r + 1], 0.0)), 0.0)
        lower_ref[r * C : (r + 1) * C, :] = lower
        scores = mm_nt(q, k) * lower
        out = mm(parts(scores, 1), twice(v, 0))
        if r > 0:
            out = out + jnp.exp(down) * mm(twice(q, 1), parts(state, 0))
        out_ref[r * C : (r + 1) * C, :] = out
        qt_ref[:, r * C : (r + 1) * C] = flipped(q).astype(BF16)
        starts_ref[r * C : (r + 1) * C, :] = state
        if r < n - 1:
            kw = flipped(k) * jnp.exp(after[r : r + 1])
            state = jnp.exp(tot[r]) * state + mm(parts(kw, 1), twice(v, 0))


def turned_kernel(q_ref, k_ref, downs_ref, rows_ref, order_ref, scores_ref, upper_ref):
    n = rows_ref.shape[0] // 5
    row = lax.broadcasted_iota(jnp.int32, (C, C), 0)
    col = lax.broadcasted_iota(jnp.int32, (C, C), 1)
    for r in range(n):
        decay = jnp.exp(jnp.minimum(rows_ref[r : r + 1, :] - chunk(downs_ref, r), 0.0))
        upper = jnp.where(row <= col, decay, 0.0)
        upper_ref[r * C : (r + 1) * C, :] = upper
        scores_ref[r * C : (r + 1) * C, :] = parts(mm_nt(chunk(k_ref, r), chunk(q_ref, r)) * upper, 1)


def back_weights(levels, count, payloads):
    own, others = payloads[: len(levels)], payloads[len(levels) :]
    behind = jnp.zeros((1, C), F32)
    weights = []
    at = 0
    for (stride, radix, rounds, back_rounds), own_ref in zip(levels, own, strict=True):
        positions, senders = places(stride, radix, rounds), places(stride, radix, back_rounds)
        mine = positions[0]
        logs = [read_log(ref) for ref in (own_ref, *others[at : at + radix - 1])]
        at += radix - 1
        for position in senders[1:]:
            weight = jnp.exp(behind + between(logs, positions, mine, position))
            weights.append(jnp.where(position > mine, weight, 0.0))
        for position in senders:
            weights.append(jnp.exp(between(logs, positions, -1, position)))
        behind = behind + between(logs, positions, mine, radix)
    weights.append(jnp.zeros((count - len(weights), C), F32))
    return jnp.concatenate(weights, axis=0)


def norm_kernel(levels, local_ref, q_ref, qt_ref, dy_ref, lead_ref, *refs):
    received, (attn_ref, dattn_ref, incoming_ref, state_ref) = refs[:-4], refs[-4:]
    n = local_ref.shape[0] // C
    own, others = received[: len(levels)], received[len(levels) :]
    incoming = jnp.zeros((C, C), F32)
    ahead = jnp.zeros((1, C), F32)
    at = 0
    for (stride, radix, rounds, _), own_ref in zip(levels, own, strict=True):
        positions = places(stride, radix, rounds)
        mine = positions[0]
        level = [own_ref, *others[at : at + radix - 1]]
        at += radix - 1
        logs = [read_log(ref) for ref in level]
        for ref, position in zip(level[1:], positions[1:], strict=True):
            weight = jnp.where(position < mine, jnp.exp(ahead + between(logs, positions, position, mine)), 0.0)
            incoming = incoming + weight * ref[:C, :].astype(F32)
        ahead = ahead + between(logs, positions, -1, mine)
    incoming_ref[...] = incoming
    incoming = incoming.astype(BF16)
    state = jnp.zeros((C, C), F32)
    for r in range(n):
        lead = chunk(lead_ref, r)
        attention = chunk(local_ref, r) + lead * mm(chunk(q_ref, r), incoming)
        dy = chunk(dy_ref, r).astype(F32)
        ratio = lax.rsqrt(jnp.mean(attention * attention, axis=1, keepdims=True) + NORM_EPS)
        along = jnp.sum(dy * attention, axis=1, keepdims=True)
        attn_ref[r * C : (r + 1) * C, :] = (attention * ratio).astype(BF16)
        dattn = ratio * dy - (ratio * ratio * ratio / C * along) * attention
        dattn_ref[r * C : (r + 1) * C, :] = dattn
        state = state + mm(qt_ref[:, r * C : (r + 1) * C], (lead * dattn).astype(BF16))
    state_ref[...] = state.astype(BF16)


def fold_back_kernel(first, radix, own_ref, *refs):
    weights_ref, out_ref = refs[radix - 1], refs[-1]
    total = jnp.zeros((C, C), F32)
    for i, ref in enumerate((own_ref, *refs[: radix - 1])):
        total = total + weights_ref[first + i : first + i + 1, :] * ref[...].astype(F32)
    out_ref[...] = total.astype(BF16)


def queries_kernel(
    levels, count, columns, stride, k_ref, v_ref, downs_ref, rows_ref, starts_ref, lower_ref, dattn_ref, incoming_ref, order_ref, *refs
):
    attn_ref, have_ref, came_ref, *payloads = refs[:-7]
    attn_hbm, dq_hbm, total_hbm, weights_ref, dq_ref, total_ref, sems = refs[-7:]
    n = rows_ref.shape[0] // 5
    copies = [
        pltpu.make_async_copy(source, target, sems.at[i])
        for i, (source, target) in enumerate(((attn_ref, attn_hbm), (total_ref, total_hbm), (dq_ref, dq_hbm)))
    ]
    copies[0].start()
    total_ref[...] = half(have_ref, columns, bit(stride), 0).astype(F32) + came_ref[...].astype(F32)
    copies[1].start()
    incoming = incoming_ref[...]
    for r in range(n):
        pair = parts(chunk(dattn_ref, r), 1)
        dscores = mm_nt(pair, twice(chunk(v_ref, r), 1)) * chunk(lower_ref, r)
        start = chunk(starts_ref, r) + rows_ref[2 * n + r : 2 * n + r + 1, :] * incoming
        dq = mm(parts(dscores, 1), twice(chunk(k_ref, r), 0))
        dq = dq + jnp.exp(chunk(downs_ref, r)) * mm_nt(pair, twice(start.astype(BF16), 1))
        dq_ref[r * C : (r + 1) * C, :] = dq.astype(BF16)
    copies[2].start()
    weights_ref[...] = back_weights(levels, count, payloads)
    for copy in copies:
        copy.wait()


def keys_kernel(
    q_ref, k_ref, v_ref, qt_ref, downs_ref, rows_ref, scores_ref, upper_ref, dattn_ref, order_ref, dk_ref, dv_ref, tail_ref
):
    n = rows_ref.shape[0] // 5
    future = jnp.zeros((C, C), F32)
    for r in reversed(range(n)):
        k, v = chunk(k_ref, r), chunk(v_ref, r)
        dattn = chunk(dattn_ref, r)
        pair = parts(dattn, 1)
        down = chunk(downs_ref, r)
        left = jnp.minimum(rows_ref[3 * n + r : 3 * n + r + 1, :] - down, 0.0)
        tail_ref[r * C : (r + 1) * C, :] = jnp.exp(left + rows_ref[4 * n + r : 4 * n + r + 1, :])
        dscores_t = mm_nt(twice(v, 1), pair) * chunk(upper_ref, r)
        scores = chunk(scores_ref, r)
        dk = mm(parts(dscores_t, 1), twice(chunk(q_ref, r), 0))
        dv = mm(scores, twice(pair[:, :C], 0)) + mm(scores[:, :C], pair[:, C:])
        if r < n - 1:
            tail = jnp.exp(left)
            dk = dk + tail * mm_nt(twice(v, 1), parts(future, 1))
            dv = dv + tail * mm(twice(k, 1), parts(future, 0))
        dk_ref[r * C : (r + 1) * C, :] = dk
        dv_ref[r * C : (r + 1) * C, :] = dv
        if r > 0:
            both = mm(qt_ref[:, r * C : (r + 1) * C], parts(jnp.exp(down) * dattn, 1))
            future = rows_ref[n + r : n + r + 1, :] * future + both[:, :C] + both[:, C:]


def last_kernel(levels, dk_ref, dv_ref, k_ref, v_ref, tail_ref, weights_ref, *refs):
    received, (k_hbm, v_hbm, out_k_ref, out_v_ref, sems) = refs[:-5], refs[-5:]
    n = dk_ref.shape[0] // C
    future = jnp.zeros((C, C), F32)
    at, taken = 0, 0
    for _, radix, _, _ in levels:
        for d in range(radix - 1):
            future = future + weights_ref[at + d : at + d + 1, :] * received[taken + d][...].astype(F32)
        at += 2 * radix - 1
        taken += radix - 1
    future = future.astype(BF16)
    copies = []
    for r in range(n):
        tail = chunk(tail_ref, r)
        dk = chunk(dk_ref, r) + tail * mm_nt(chunk(v_ref, r), future)
        out_k_ref[r * C : (r + 1) * C, :] = dk.astype(BF16)
        dv = chunk(dv_ref, r) + tail * mm(chunk(k_ref, r), future)
        out_v_ref[r * C : (r + 1) * C, :] = dv.astype(BF16)
        if (r + 1) % (n // 2) == 0:
            rows = pl.ds((r + 1 - n // 2) * C, n // 2 * C)
            for source, target in ((out_k_ref, k_hbm), (out_v_ref, v_hbm)):
                copies.append(pltpu.make_async_copy(source.at[rows], target.at[rows], sems.at[len(copies)]))
                copies[-1].start()
    for copy in copies:
        copy.wait()


def half(ref, columns, odd, i):
    return ref[:, pl.ds(pl.multiple_of((2 * i + odd) * columns, C), columns)]


def bit(stride):
    return lax.rem(lax.div(lax.axis_index("dp"), stride), 2)


def cut_kernel(columns, have_ref, order_ref, sent_ref):
    for i in range(have_ref.shape[1] // columns // 2):
        sent_ref[:, i * columns : (i + 1) * columns] = half(have_ref, columns, 1 - bit(1), i)


def add_kernel(columns, stride, have_ref, came_ref, kept_ref, sent_ref):
    for i in range(have_ref.shape[1] // columns // 2):
        kept = half(have_ref, columns, bit(stride), i).astype(F32)
        kept_ref[:, i * columns : (i + 1) * columns] = kept + came_ref[:, i * columns : (i + 1) * columns].astype(F32)
    for i in range(kept_ref.shape[1] // columns // 2):
        sent_ref[:, i * columns : (i + 1) * columns] = half(kept_ref, columns, 1 - bit(2 * stride), i).astype(BF16)


def call(body, shapes, name, scratch=(), in_specs=None, out_specs=None, flops=0, moved=1024, vmem=32 << 20):
    specs = {}
    if in_specs is not None:
        specs["in_specs"] = in_specs
    if out_specs is not None:
        specs["out_specs"] = out_specs
    return pl.pallas_call(
        body,
        out_shape=shapes,
        scratch_shapes=scratch,
        name=name,
        compiler_params=pltpu.CompilerParams(vmem_limit_bytes=vmem),
        cost_estimate=pl.CostEstimate(flops=flops, bytes_accessed=moved, transcendentals=0),
        **specs,
    )


def rounds_of(stride, places_to):
    return tuple(
        tuple(targets[at // stride] * stride + at % stride for at in range(stride * len(targets))) for targets in places_to
    )


def scan_levels(size):
    levels, stride = [], 1
    while stride < size:
        radix = 2 if stride == 1 else min(4, size // stride)
        pairs = tuple(tuple(at ^ d for at in range(radix)) for d in range(1, radix))
        forward = rounds_of(stride, FORWARD_OF_4 if radix == 4 else pairs)
        backward = rounds_of(stride, LAST_BACKWARD_OF_4 if radix == 4 and 4 * stride == size else pairs)
        levels.append((stride, radix, forward, backward))
        stride *= radix
    return levels


def send(x, axis, size, targets):
    pairs = [(i, i - i % len(targets) + targets[i % len(targets)]) for i in range(size)]
    return lax.ppermute(x, axis, pairs)


def local(levels, seq, dp, queries, key_vectors, value_vectors, out_grad, log_decay, prev_grads):
    q, k, v, dy = queries[0], key_vectors[0], value_vectors[0], out_grad[0]
    tokens = q.shape[0]
    n = tokens // C
    decay = log_decay.reshape(n, C)
    shape = jax.ShapeDtypeStruct
    payload = shape((C + LOGS, C), BF16)
    square = shape((C, C), F32)
    wide, narrow = shape((tokens, C), F32), shape((tokens, C), BF16)

    away = pl.BlockSpec(memory_space=pltpu.HBM)
    here = pl.BlockSpec(memory_space=pltpu.VMEM)
    whole = pltpu.VMEM((tokens, C), BF16)
    dma = pltpu.SemaphoreType.DMA

    own = [
        call(
            state_kernel,
            payload,
            "state",
            scratch=[whole, whole, pltpu.VMEM((n, C), F32), dma((3,))],
            in_specs=[away] * 3,
        )(*[pltpu.with_memory_space_constraint(x, pltpu.HBM) for x in (k, v, decay)])
    ]
    grads = prev_grads[0]
    lines = grads.shape[0]
    columns = grads.shape[1] // dp
    others = []
    for i, (stride, radix, rounds, _) in enumerate(levels):
        got = [send(own[-1], "seq", seq, targets) for targets in rounds]
        others += got
        if i == 0:
            sent = call(functools.partial(cut_kernel, columns), shape((lines, grads.shape[1] // 2), BF16), "cut")(grads, own[0])
            came = send(sent, "dp", dp, (1, 0))
            total, part = grads, 1
            while 2 * part < dp:
                kept, sent = shape((lines, total.shape[1] // 2), F32), shape((lines, total.shape[1] // 4), BF16)
                total, sent = call(functools.partial(add_kernel, columns, part), (kept, sent), "add")(total, came)
                part *= 2
                came = send(sent, "dp", dp, rounds_of(part, ((1, 0),))[0])
        if i < len(levels) - 1:
            fold = functools.partial(fold_kernel, stride, radix, rounds)
            own.append(call(fold, payload, "fold")(own[-1], *got, *([total] if i == 0 else [])))
    local_out, downs, rows, qt, starts, lower, lead = call(
        forward_kernel, (wide, wide, shape((5 * n, C), F32), shape((C, tokens), BF16), wide, wide, wide), "forward"
    )(q, k, v, decay, own[-1], dy)
    scores_t, upper = call(turned_kernel, (shape((tokens, 2 * C), BF16), wide), "turned")(q, k, downs, rows, own[-1])
    count = sum(2 * radix - 1 for _, radix, _, _ in levels)
    count += -count % 8
    attention, dattn, incoming, state = call(
        functools.partial(norm_kernel, levels), (narrow, wide, square, shape((C, C), BF16)), "norm"
    )(local_out, q, qt, dy, lead, *own, *others, scores_t)

    attn_out, grad_query, grad_shard, weights = call(
        functools.partial(queries_kernel, levels, count, columns, dp // 2),
        (narrow, narrow, shape((lines, columns), F32), shape((count, C), F32)),
        "queries",
        scratch=[whole, pltpu.VMEM((lines, columns), F32), dma((3,))],
        in_specs=[here] * (12 + len(own) + len(others)),
        out_specs=(away, away, away, here),
    )(k, v, downs, rows, starts, lower, dattn, incoming, state, attention, total, came, *own, *others)
    received = []
    at = 0
    for i, (stride, radix, _, rounds) in enumerate(levels):
        got = [send(state, "seq", seq, targets) for targets in rounds]
        received += got
        if i < len(levels) - 1:
            fold = functools.partial(fold_back_kernel, at + radix - 1, radix)
            state = call(fold, shape((C, C), BF16), "fold_back")(state, *got, weights)
        at += 2 * radix - 1
    dk, dv, tail = call(keys_kernel, (wide, wide, wide), "keys")(q, k, v, qt, downs, rows, scores_t, upper, dattn, state)
    grad_key, grad_value = call(
        functools.partial(last_kernel, levels),
        (narrow, narrow),
        "last",
        scratch=[whole, whole, dma((4,))],
        in_specs=[here] * (6 + len(received)),
        out_specs=(away, away),
    )(dk, dv, k, v, tail, weights, *received)
    return attn_out[None], grad_query[None], grad_key[None], grad_value[None], grad_shard


def solution(mesh):
    seq, dp = mesh.shape["seq"], mesh.shape["dp"]
    return jax.shard_map(
        functools.partial(local, scan_levels(seq), seq, dp),
        mesh=mesh,
        in_specs=(
            P("dp", "seq", None),
            P("dp", "seq", None),
            P("dp", "seq", None),
            P("dp", "seq", None),
            P("dp", None, "seq"),
            P("dp", "seq", None),
        ),
        out_specs=(
            P("dp", "seq", None),
            P("dp", "seq", None),
            P("dp", "seq", None),
            P("dp", "seq", None),
            P("seq", "dp"),
        ),
        check_vma=False,
    )
```

```python
import functools

import jax
import jax.numpy as jnp
from jax import lax
from jax.experimental import pallas as pl
from jax.experimental.pallas import tpu as pltpu
from jax.sharding import PartitionSpec as P

NORM_EPS = 1e-06
C = 128
F32 = jnp.float32
BF16 = jnp.bfloat16
FORWARD_OF_4 = ((3, 0, 1, 2), (2, 3, 0, 1), (1, 2, 3, 0))
LAST_BACKWARD_OF_4 = ((1, 0, 3, 2), (2, 3, 0, 1), (2, 3, 1, 0))
LOGS = 16


def mm(a, b):
    return lax.dot_general(a, b, (((1,), (0,)), ((), ())), preferred_element_type=F32)


def mm_nt(a, b):
    return lax.dot_general(a, b, (((1,), (1,)), ((), ())), preferred_element_type=F32)


def split(x):
    high = x.astype(BF16)
    return high, (x - high.astype(F32)).astype(BF16)


def twice(x, axis):
    return jnp.concatenate([x, x], axis=axis)


def parts(x, axis):
    return jnp.concatenate(split(x), axis=axis)


def cut3(x):
    high = x.astype(BF16).astype(F32)
    middle = (x - high).astype(BF16).astype(F32)
    return high, middle, x - high - middle


def sums(decay):
    n = decay.shape[0]
    row = lax.broadcasted_iota(jnp.int32, (C, C), 0)
    col = lax.broadcasted_iota(jnp.int32, (C, C), 1)
    upto = (row <= col).astype(F32)
    after = (row > col).astype(F32)
    ones = jnp.concatenate([upto, after], axis=1).astype(BF16)
    pieces = jnp.concatenate(cut3(decay), axis=0).astype(BF16)
    both = mm(pieces, ones)
    both = both[:n] + both[n : 2 * n] + both[2 * n :]
    return both[:, :C], both[:, C:]


def totals(upto):
    n = upto.shape[0]
    return [jnp.broadcast_to(upto[r : r + 1, C - 1 :], (1, C)) for r in range(n)]


def before_chunks(tot):
    out = [jnp.zeros((1, C), F32)]
    for t in tot[:-1]:
        out.append(out[-1] + t)
    return out


def after_chunks(tot):
    return before_chunks(tot[::-1])[::-1]


def chunk(ref, r):
    return ref[r * C : (r + 1) * C, :]


def flipped(x):
    return x.astype(F32).T


def log_rows(total):
    high, middle, low = cut3(total)
    return jnp.concatenate([high, middle, low, jnp.zeros((LOGS - 3, C), F32)], axis=0).astype(BF16)


def read_log(ref):
    rows = ref[C:, :].astype(F32)
    return rows[0:1] + rows[1:2] + rows[2:3]


def state_kernel(columns, k_hbm, v_hbm, decay_hbm, grads_hbm, out_ref, sent_ref, k_ref, v_ref, decay_ref, sems):
    pairs = [(decay_hbm, decay_ref), (k_hbm, k_ref), (v_hbm, v_ref)]
    for i in range(grads_hbm.shape[1] // columns // 2):
        block = grads_hbm.at[:, pl.ds(pl.multiple_of((2 * i + 1 - bit(1)) * columns, C), columns)]
        pairs.append((block, sent_ref.at[:, pl.ds(i * columns, columns)]))
    copies = [pltpu.make_async_copy(source, target, sems.at[i]) for i, (source, target) in enumerate(pairs)]
    for copy in copies:
        copy.start()
    copies[0].wait()
    upto, after = sums(decay_ref[...])
    tot = totals(upto)
    later = after_chunks(tot)
    weights = [jnp.exp(after[r : r + 1] + later[r]) for r in range(len(tot))]
    copies[1].wait()
    copies[2].wait()
    state = jnp.zeros((C, C), F32)
    for r, weight in enumerate(weights):
        kw = flipped(chunk(k_ref, r)) * weight
        state = state + mm(kw.astype(BF16), chunk(v_ref, r))
    out_ref[:C, :] = state.astype(BF16)
    out_ref[C:, :] = log_rows(sum(tot))
    for copy in copies[3:]:
        copy.wait()


def between(logs, positions, low, high):
    out = jnp.zeros((1, C), F32)
    for log, position in zip(logs, positions, strict=True):
        out = out + jnp.where((position > low) & (position < high), log, 0.0)
    return out


def places(stride, radix, rounds):
    block = lax.rem(lax.axis_index("seq"), stride * radix)
    senders = [sum(jnp.where(block == to, at // stride, 0) for at, to in enumerate(targets)) for targets in rounds]
    return [lax.div(block, stride), *senders]


def fold_kernel(stride, radix, rounds, own_ref, *refs):
    out_ref = refs[-1]
    positions = places(stride, radix, rounds)
    all_refs = [own_ref, *refs[: radix - 1]]
    logs = [read_log(ref) for ref in all_refs]
    total = jnp.zeros((C, C), F32)
    for ref, position in zip(all_refs, positions, strict=True):
        weight = jnp.exp(between(logs, positions, position, radix))
        total = total + weight * ref[:C, :].astype(F32)
    out_ref[:C, :] = total.astype(BF16)
    out_ref[C:, :] = log_rows(sum(logs))


def spread(decay_row):
    row = lax.broadcasted_iota(jnp.int32, (C, C), 0)
    col = lax.broadcasted_iota(jnp.int32, (C, C), 1)
    pieces = jnp.concatenate([jnp.where(row >= col, x, 0.0) for x in cut3(decay_row)], axis=1).astype(BF16)
    return mm(pieces, jnp.ones((3 * C, C), BF16))


def forward_kernel(
    q_ref, k_ref, v_ref, decay_ref, order_ref, dy_ref, out_ref, downs_ref, rows_ref, qt_ref, starts_ref, lower_ref, lead_ref
):
    upto, after = sums(decay_ref[...])
    tot = totals(upto)
    begin, later = before_chunks(tot), after_chunks(tot)
    n = len(tot)
    row = lax.broadcasted_iota(jnp.int32, (C, C), 0)
    col = lax.broadcasted_iota(jnp.int32, (C, C), 1)
    rows_ref[:n, :] = upto
    for i, rows in enumerate(([jnp.exp(x) for x in tot], [jnp.exp(x) for x in begin], tot, later), 1):
        rows_ref[i * n : (i + 1) * n, :] = jnp.concatenate(rows, axis=0)
    state = jnp.zeros((C, C), F32)
    for r in range(n):
        q, k, v = chunk(q_ref, r), chunk(k_ref, r), chunk(v_ref, r)
        down = spread(decay_ref[r : r + 1, :])
        downs_ref[r * C : (r + 1) * C, :] = down
        lead_ref[r * C : (r + 1) * C, :] = jnp.exp(down + begin[r])
        lower = jnp.where(row >= col, jnp.exp(jnp.minimum(down - upto[r : r + 1], 0.0)), 0.0)
        lower_ref[r * C : (r + 1) * C, :] = lower
        scores = mm_nt(q, k) * lower
        out = mm(parts(scores, 1), twice(v, 0))
        if r > 0:
            out = out + jnp.exp(down) * mm(twice(q, 1), parts(state, 0))
        out_ref[r * C : (r + 1) * C, :] = out
        qt_ref[:, r * C : (r + 1) * C] = flipped(q).astype(BF16)
        starts_ref[r * C : (r + 1) * C, :] = state
        if r < n - 1:
            kw = flipped(k) * jnp.exp(after[r : r + 1])
            state = jnp.exp(tot[r]) * state + mm(parts(kw, 1), twice(v, 0))


def turned_kernel(q_ref, k_ref, downs_ref, rows_ref, order_ref, scores_ref, upper_ref):
    n = rows_ref.shape[0] // 5
    row = lax.broadcasted_iota(jnp.int32, (C, C), 0)
    col = lax.broadcasted_iota(jnp.int32, (C, C), 1)
    for r in range(n):
        decay = jnp.exp(jnp.minimum(rows_ref[r : r + 1, :] - chunk(downs_ref, r), 0.0))
        upper = jnp.where(row <= col, decay, 0.0)
        upper_ref[r * C : (r + 1) * C, :] = upper
        scores_ref[r * C : (r + 1) * C, :] = parts(mm_nt(chunk(k_ref, r), chunk(q_ref, r)) * upper, 1)


def back_weights(levels, count, payloads):
    own, others = payloads[: len(levels)], payloads[len(levels) :]
    behind = jnp.zeros((1, C), F32)
    weights = []
    at = 0
    for (stride, radix, rounds, back_rounds), own_ref in zip(levels, own, strict=True):
        positions, senders = places(stride, radix, rounds), places(stride, radix, back_rounds)
        mine = positions[0]
        logs = [read_log(ref) for ref in (own_ref, *others[at : at + radix - 1])]
        at += radix - 1
        for position in senders[1:]:
            weight = jnp.exp(behind + between(logs, positions, mine, position))
            weights.append(jnp.where(position > mine, weight, 0.0))
        for position in senders:
            weights.append(jnp.exp(between(logs, positions, -1, position)))
        behind = behind + between(logs, positions, mine, radix)
    weights.append(jnp.zeros((count - len(weights), C), F32))
    return jnp.concatenate(weights, axis=0)


def norm_kernel(levels, local_ref, q_ref, qt_ref, dy_ref, lead_ref, *refs):
    received, (attn_ref, dattn_ref, incoming_ref, state_ref) = refs[:-4], refs[-4:]
    n = local_ref.shape[0] // C
    own, others = received[: len(levels)], received[len(levels) :]
    incoming = jnp.zeros((C, C), F32)
    ahead = jnp.zeros((1, C), F32)
    at = 0
    for (stride, radix, rounds, _), own_ref in zip(levels, own, strict=True):
        positions = places(stride, radix, rounds)
        mine = positions[0]
        level = [own_ref, *others[at : at + radix - 1]]
        at += radix - 1
        logs = [read_log(ref) for ref in level]
        for ref, position in zip(level[1:], positions[1:], strict=True):
            weight = jnp.where(position < mine, jnp.exp(ahead + between(logs, positions, position, mine)), 0.0)
            incoming = incoming + weight * ref[:C, :].astype(F32)
        ahead = ahead + between(logs, positions, -1, mine)
    incoming_ref[...] = incoming
    incoming = incoming.astype(BF16)
    state = jnp.zeros((C, C), F32)
    for r in range(n):
        lead = chunk(lead_ref, r)
        attention = chunk(local_ref, r) + lead * mm(chunk(q_ref, r), incoming)
        dy = chunk(dy_ref, r).astype(F32)
        ratio = lax.rsqrt(jnp.mean(attention * attention, axis=1, keepdims=True) + NORM_EPS)
        along = jnp.sum(dy * attention, axis=1, keepdims=True)
        attn_ref[r * C : (r + 1) * C, :] = (attention * ratio).astype(BF16)
        dattn = ratio * dy - (ratio * ratio * ratio / C * along) * attention
        dattn_ref[r * C : (r + 1) * C, :] = dattn
        state = state + mm(qt_ref[:, r * C : (r + 1) * C], (lead * dattn).astype(BF16))
    state_ref[...] = state.astype(BF16)


def fold_back_kernel(first, radix, own_ref, *refs):
    weights_ref, out_ref = refs[radix - 1], refs[-1]
    total = jnp.zeros((C, C), F32)
    for i, ref in enumerate((own_ref, *refs[: radix - 1])):
        total = total + weights_ref[first + i : first + i + 1, :] * ref[...].astype(F32)
    out_ref[...] = total.astype(BF16)


def queries_kernel(
    levels, count, columns, stride, k_ref, v_ref, downs_ref, rows_ref, starts_ref, lower_ref, dattn_ref, incoming_ref, order_ref, *refs
):
    attn_ref, have_ref, came_ref, *payloads = refs[:-7]
    attn_hbm, dq_hbm, total_hbm, weights_ref, dq_ref, total_ref, sems = refs[-7:]
    n = rows_ref.shape[0] // 5
    copies = [
        pltpu.make_async_copy(source, target, sems.at[i])
        for i, (source, target) in enumerate(((attn_ref, attn_hbm), (total_ref, total_hbm), (dq_ref, dq_hbm)))
    ]
    copies[0].start()
    total_ref[...] = half(have_ref, columns, bit(stride), 0).astype(F32) + came_ref[...].astype(F32)
    copies[1].start()
    incoming = incoming_ref[...]
    for r in range(n):
        pair = parts(chunk(dattn_ref, r), 1)
        dscores = mm_nt(pair, twice(chunk(v_ref, r), 1)) * chunk(lower_ref, r)
        start = chunk(starts_ref, r) + rows_ref[2 * n + r : 2 * n + r + 1, :] * incoming
        dq = mm(parts(dscores, 1), twice(chunk(k_ref, r), 0))
        dq = dq + jnp.exp(chunk(downs_ref, r)) * mm_nt(pair, twice(start.astype(BF16), 1))
        dq_ref[r * C : (r + 1) * C, :] = dq.astype(BF16)
    copies[2].start()
    weights_ref[...] = back_weights(levels, count, payloads)
    for copy in copies:
        copy.wait()


def keys_kernel(
    q_ref, k_ref, v_ref, qt_ref, downs_ref, rows_ref, scores_ref, upper_ref, dattn_ref, order_ref, dk_ref, dv_ref, tail_ref
):
    n = rows_ref.shape[0] // 5
    future = jnp.zeros((C, C), F32)
    for r in reversed(range(n)):
        k, v = chunk(k_ref, r), chunk(v_ref, r)
        dattn = chunk(dattn_ref, r)
        pair = parts(dattn, 1)
        down = chunk(downs_ref, r)
        left = jnp.minimum(rows_ref[3 * n + r : 3 * n + r + 1, :] - down, 0.0)
        tail_ref[r * C : (r + 1) * C, :] = jnp.exp(left + rows_ref[4 * n + r : 4 * n + r + 1, :])
        dscores_t = mm_nt(twice(v, 1), pair) * chunk(upper_ref, r)
        scores = chunk(scores_ref, r)
        dk = mm(parts(dscores_t, 1), twice(chunk(q_ref, r), 0))
        dv = mm(scores, twice(pair[:, :C], 0)) + mm(scores[:, :C], pair[:, C:])
        if r < n - 1:
            tail = jnp.exp(left)
            dk = dk + tail * mm_nt(twice(v, 1), parts(future, 1))
            dv = dv + tail * mm(twice(k, 1), parts(future, 0))
        dk_ref[r * C : (r + 1) * C, :] = dk
        dv_ref[r * C : (r + 1) * C, :] = dv
        if r > 0:
            both = mm(qt_ref[:, r * C : (r + 1) * C], parts(jnp.exp(down) * dattn, 1))
            future = rows_ref[n + r : n + r + 1, :] * future + both[:, :C] + both[:, C:]


def last_kernel(levels, dk_ref, dv_ref, k_ref, v_ref, tail_ref, weights_ref, *refs):
    received, (k_hbm, v_hbm, out_k_ref, out_v_ref, sems) = refs[:-5], refs[-5:]
    n = dk_ref.shape[0] // C
    future = jnp.zeros((C, C), F32)
    at, taken = 0, 0
    for _, radix, _, _ in levels:
        for d in range(radix - 1):
            future = future + weights_ref[at + d : at + d + 1, :] * received[taken + d][...].astype(F32)
        at += 2 * radix - 1
        taken += radix - 1
    future = future.astype(BF16)
    copies = []
    for r in range(n):
        tail = chunk(tail_ref, r)
        dk = chunk(dk_ref, r) + tail * mm_nt(chunk(v_ref, r), future)
        out_k_ref[r * C : (r + 1) * C, :] = dk.astype(BF16)
        dv = chunk(dv_ref, r) + tail * mm(chunk(k_ref, r), future)
        out_v_ref[r * C : (r + 1) * C, :] = dv.astype(BF16)
        if (r + 1) % (n // 2) == 0:
            rows = pl.ds((r + 1 - n // 2) * C, n // 2 * C)
            for source, target in ((out_k_ref, k_hbm), (out_v_ref, v_hbm)):
                copies.append(pltpu.make_async_copy(source.at[rows], target.at[rows], sems.at[len(copies)]))
                copies[-1].start()
    for copy in copies:
        copy.wait()


def half(ref, columns, odd, i):
    return ref[:, pl.ds(pl.multiple_of((2 * i + odd) * columns, C), columns)]


def bit(stride):
    return lax.rem(lax.div(lax.axis_index("dp"), stride), 2)


def add_kernel(columns, stride, have_ref, came_ref, kept_ref, sent_ref):
    for i in range(have_ref.shape[1] // columns // 2):
        kept = half(have_ref, columns, bit(stride), i).astype(F32)
        kept_ref[:, i * columns : (i + 1) * columns] = kept + came_ref[:, i * columns : (i + 1) * columns].astype(F32)
    for i in range(kept_ref.shape[1] // columns // 2):
        sent_ref[:, i * columns : (i + 1) * columns] = half(kept_ref, columns, 1 - bit(2 * stride), i).astype(BF16)


def call(body, shapes, name, scratch=(), in_specs=None, out_specs=None, flops=0, moved=1024, vmem=32 << 20):
    specs = {}
    if in_specs is not None:
        specs["in_specs"] = in_specs
    if out_specs is not None:
        specs["out_specs"] = out_specs
    return pl.pallas_call(
        body,
        out_shape=shapes,
        scratch_shapes=scratch,
        name=name,
        compiler_params=pltpu.CompilerParams(vmem_limit_bytes=vmem),
        cost_estimate=pl.CostEstimate(flops=flops, bytes_accessed=moved, transcendentals=0),
        **specs,
    )


def rounds_of(stride, places_to):
    return tuple(
        tuple(targets[at // stride] * stride + at % stride for at in range(stride * len(targets))) for targets in places_to
    )


def scan_levels(size):
    levels, stride = [], 1
    while stride < size:
        radix = 2 if stride == 1 else min(4, size // stride)
        pairs = tuple(tuple(at ^ d for at in range(radix)) for d in range(1, radix))
        forward = rounds_of(stride, FORWARD_OF_4 if radix == 4 else pairs)
        backward = rounds_of(stride, LAST_BACKWARD_OF_4 if radix == 4 and 4 * stride == size else pairs)
        levels.append((stride, radix, forward, backward))
        stride *= radix
    return levels


def send(x, axis, size, targets):
    pairs = [(i, i - i % len(targets) + targets[i % len(targets)]) for i in range(size)]
    return lax.ppermute(x, axis, pairs)


def local(levels, seq, dp, queries, key_vectors, value_vectors, out_grad, log_decay, prev_grads):
    q, k, v, dy = queries[0], key_vectors[0], value_vectors[0], out_grad[0]
    tokens = q.shape[0]
    n = tokens // C
    decay = log_decay.reshape(n, C)
    shape = jax.ShapeDtypeStruct
    payload = shape((C + LOGS, C), BF16)
    square = shape((C, C), F32)
    wide, narrow = shape((tokens, C), F32), shape((tokens, C), BF16)

    away = pl.BlockSpec(memory_space=pltpu.HBM)
    here = pl.BlockSpec(memory_space=pltpu.VMEM)
    whole = pltpu.VMEM((tokens, C), BF16)
    dma = pltpu.SemaphoreType.DMA

    grads = prev_grads[0]
    lines = grads.shape[0]
    columns = grads.shape[1] // dp
    state, sent = call(
        functools.partial(state_kernel, columns),
        (payload, shape((lines, grads.shape[1] // 2), BF16)),
        "state",
        scratch=[whole, whole, pltpu.VMEM((n, C), F32), dma((3 + dp // 2,))],
        in_specs=[away] * 4,
    )(*[pltpu.with_memory_space_constraint(x, pltpu.HBM) for x in (k, v, decay, grads)])
    own = [state]
    others = []
    for i, (stride, radix, rounds, _) in enumerate(levels):
        got = [send(own[-1], "seq", seq, targets) for targets in rounds]
        others += got
        if i == 0:
            came = send(sent, "dp", dp, (1, 0))
            total, part = grads, 1
            while 2 * part < dp:
                kept, sent = shape((lines, total.shape[1] // 2), F32), shape((lines, total.shape[1] // 4), BF16)
                total, sent = call(functools.partial(add_kernel, columns, part), (kept, sent), "add")(total, came)
                part *= 2
                came = send(sent, "dp", dp, rounds_of(part, ((1, 0),))[0])
        if i < len(levels) - 1:
            fold = functools.partial(fold_kernel, stride, radix, rounds)
            own.append(call(fold, payload, "fold")(own[-1], *got, *([total] if i == 0 else [])))
    local_out, downs, rows, qt, starts, lower, lead = call(
        forward_kernel, (wide, wide, shape((5 * n, C), F32), shape((C, tokens), BF16), wide, wide, wide), "forward"
    )(q, k, v, decay, own[-1], dy)
    scores_t, upper = call(turned_kernel, (shape((tokens, 2 * C), BF16), wide), "turned")(q, k, downs, rows, own[-1])
    count = sum(2 * radix - 1 for _, radix, _, _ in levels)
    count += -count % 8
    attention, dattn, incoming, state = call(
        functools.partial(norm_kernel, levels), (narrow, wide, square, shape((C, C), BF16)), "norm"
    )(local_out, q, qt, dy, lead, *own, *others, scores_t)

    attn_out, grad_query, grad_shard, weights = call(
        functools.partial(queries_kernel, levels, count, columns, dp // 2),
        (narrow, narrow, shape((lines, columns), F32), shape((count, C), F32)),
        "queries",
        scratch=[whole, pltpu.VMEM((lines, columns), F32), dma((3,))],
        in_specs=[here] * (12 + len(own) + len(others)),
        out_specs=(away, away, away, here),
    )(k, v, downs, rows, starts, lower, dattn, incoming, state, attention, total, came, *own, *others)
    received = []
    at = 0
    for i, (stride, radix, _, rounds) in enumerate(levels):
        got = [send(state, "seq", seq, targets) for targets in rounds]
        received += got
        if i < len(levels) - 1:
            fold = functools.partial(fold_back_kernel, at + radix - 1, radix)
            state = call(fold, shape((C, C), BF16), "fold_back")(state, *got, weights)
        at += 2 * radix - 1
    dk, dv, tail = call(keys_kernel, (wide, wide, wide), "keys")(q, k, v, qt, downs, rows, scores_t, upper, dattn, state)
    grad_key, grad_value = call(
        functools.partial(last_kernel, levels),
        (narrow, narrow),
        "last",
        scratch=[whole, whole, dma((4,))],
        in_specs=[here] * (6 + len(received)),
        out_specs=(away, away),
    )(dk, dv, k, v, tail, weights, *received)
    return attn_out[None], grad_query[None], grad_key[None], grad_value[None], grad_shard


def solution(mesh):
    seq, dp = mesh.shape["seq"], mesh.shape["dp"]
    return jax.shard_map(
        functools.partial(local, scan_levels(seq), seq, dp),
        mesh=mesh,
        in_specs=(
            P("dp", "seq", None),
            P("dp", "seq", None),
            P("dp", "seq", None),
            P("dp", "seq", None),
            P("dp", None, "seq"),
            P("dp", "seq", None),
        ),
        out_specs=(
            P("dp", "seq", None),
            P("dp", "seq", None),
            P("dp", "seq", None),
            P("dp", "seq", None),
            P("seq", "dp"),
        ),
        check_vma=False,
    )
```

```python
import functools

import jax
import jax.numpy as jnp
from jax import lax
from jax.experimental import pallas as pl
from jax.experimental.pallas import tpu as pltpu
from jax.sharding import PartitionSpec as P

NORM_EPS = 1e-06
C = 128
F32 = jnp.float32
BF16 = jnp.bfloat16
FORWARD_OF_4 = ((3, 0, 1, 2), (2, 3, 0, 1), (1, 2, 3, 0))
LAST_BACKWARD_OF_4 = ((1, 0, 3, 2), (2, 3, 0, 1), (2, 3, 1, 0))
LOGS = 16


def mm(a, b):
    return lax.dot_general(a, b, (((1,), (0,)), ((), ())), preferred_element_type=F32)


def mm_nt(a, b):
    return lax.dot_general(a, b, (((1,), (1,)), ((), ())), preferred_element_type=F32)


def split(x):
    high = x.astype(BF16)
    return high, (x - high.astype(F32)).astype(BF16)


def twice(x, axis):
    return jnp.concatenate([x, x], axis=axis)


def parts(x, axis):
    return jnp.concatenate(split(x), axis=axis)


def cut3(x):
    high = x.astype(BF16).astype(F32)
    middle = (x - high).astype(BF16).astype(F32)
    return high, middle, x - high - middle


def sums(decay):
    n = decay.shape[0]
    row = lax.broadcasted_iota(jnp.int32, (C, C), 0)
    col = lax.broadcasted_iota(jnp.int32, (C, C), 1)
    upto = (row <= col).astype(F32)
    after = (row > col).astype(F32)
    ones = jnp.concatenate([upto, after], axis=1).astype(BF16)
    pieces = jnp.concatenate(cut3(decay), axis=0).astype(BF16)
    both = mm(pieces, ones)
    both = both[:n] + both[n : 2 * n] + both[2 * n :]
    return both[:, :C], both[:, C:]


def totals(upto):
    n = upto.shape[0]
    return [jnp.broadcast_to(upto[r : r + 1, C - 1 :], (1, C)) for r in range(n)]


def before_chunks(tot):
    out = [jnp.zeros((1, C), F32)]
    for t in tot[:-1]:
        out.append(out[-1] + t)
    return out


def after_chunks(tot):
    return before_chunks(tot[::-1])[::-1]


def chunk(ref, r):
    return ref[r * C : (r + 1) * C, :]


def flipped(x):
    return x.astype(F32).T


def log_rows(total):
    high, middle, low = cut3(total)
    return jnp.concatenate([high, middle, low, jnp.zeros((LOGS - 3, C), F32)], axis=0).astype(BF16)


def read_log(ref):
    rows = ref[C:, :].astype(F32)
    return rows[0:1] + rows[1:2] + rows[2:3]


def state_kernel(columns, k_hbm, v_hbm, decay_hbm, grads_hbm, out_ref, sent_ref, k_ref, v_ref, decay_ref, sems):
    pairs = [(decay_hbm, decay_ref), (k_hbm, k_ref), (v_hbm, v_ref)]
    for i in range(grads_hbm.shape[1] // columns // 2):
        block = grads_hbm.at[:, pl.ds(pl.multiple_of((2 * i + 1 - bit(1)) * columns, C), columns)]
        pairs.append((block, sent_ref.at[:, pl.ds(i * columns, columns)]))
    copies = [pltpu.make_async_copy(source, target, sems.at[i]) for i, (source, target) in enumerate(pairs)]
    for copy in copies:
        copy.start()
    copies[0].wait()
    upto, after = sums(decay_ref[...])
    tot = totals(upto)
    later = after_chunks(tot)
    weights = [jnp.exp(after[r : r + 1] + later[r]) for r in range(len(tot))]
    copies[1].wait()
    copies[2].wait()
    state = jnp.zeros((C, C), F32)
    for r in range(0, len(weights), 2):
        kw = [(flipped(chunk(k_ref, i)) * weights[i]).astype(BF16) for i in (r, r + 1)]
        state = state + mm(jnp.concatenate(kw, axis=1), v_ref[r * C : (r + 2) * C, :])
    out_ref[:C, :] = state.astype(BF16)
    out_ref[C:, :] = log_rows(sum(tot))
    for copy in copies[3:]:
        copy.wait()


def between(logs, positions, low, high):
    out = jnp.zeros((1, C), F32)
    for log, position in zip(logs, positions, strict=True):
        out = out + jnp.where((position > low) & (position < high), log, 0.0)
    return out


def places(stride, radix, rounds):
    block = lax.rem(lax.axis_index("seq"), stride * radix)
    senders = [sum(jnp.where(block == to, at // stride, 0) for at, to in enumerate(targets)) for targets in rounds]
    return [lax.div(block, stride), *senders]


def fold_kernel(stride, radix, rounds, own_ref, *refs):
    out_ref = refs[-1]
    positions = places(stride, radix, rounds)
    all_refs = [own_ref, *refs[: radix - 1]]
    logs = [read_log(ref) for ref in all_refs]
    total = jnp.zeros((C, C), F32)
    for ref, position in zip(all_refs, positions, strict=True):
        weight = jnp.exp(between(logs, positions, position, radix))
        total = total + weight * ref[:C, :].astype(F32)
    out_ref[:C, :] = total.astype(BF16)
    out_ref[C:, :] = log_rows(sum(logs))


def spread(decay_row):
    row = lax.broadcasted_iota(jnp.int32, (C, C), 0)
    col = lax.broadcasted_iota(jnp.int32, (C, C), 1)
    pieces = jnp.concatenate([jnp.where(row >= col, x, 0.0) for x in cut3(decay_row)], axis=1).astype(BF16)
    return mm(pieces, jnp.ones((3 * C, C), BF16))


def forward_kernel(
    q_ref, k_ref, v_ref, decay_ref, order_ref, dy_ref, out_ref, downs_ref, rows_ref, qt_ref, starts_ref, lower_ref, lead_ref
):
    upto, after = sums(decay_ref[...])
    tot = totals(upto)
    begin, later = before_chunks(tot), after_chunks(tot)
    n = len(tot)
    row = lax.broadcasted_iota(jnp.int32, (C, C), 0)
    col = lax.broadcasted_iota(jnp.int32, (C, C), 1)
    rows_ref[:n, :] = upto
    for i, rows in enumerate(([jnp.exp(x) for x in tot], [jnp.exp(x) for x in begin], tot, later), 1):
        rows_ref[i * n : (i + 1) * n, :] = jnp.concatenate(rows, axis=0)
    state = jnp.zeros((C, C), F32)
    for r in range(n):
        q, k, v = chunk(q_ref, r), chunk(k_ref, r), chunk(v_ref, r)
        down = spread(decay_ref[r : r + 1, :])
        downs_ref[r * C : (r + 1) * C, :] = down
        lead_ref[r * C : (r + 1) * C, :] = jnp.exp(down + begin[r])
        lower = jnp.where(row >= col, jnp.exp(jnp.minimum(down - upto[r : r + 1], 0.0)), 0.0)
        lower_ref[r * C : (r + 1) * C, :] = lower
        scores = mm_nt(q, k) * lower
        out = mm(parts(scores, 1), twice(v, 0))
        if r > 0:
            out = out + jnp.exp(down) * mm(twice(q, 1), parts(state, 0))
        out_ref[r * C : (r + 1) * C, :] = out
        qt_ref[:, r * C : (r + 1) * C] = flipped(q).astype(BF16)
        starts_ref[r * C : (r + 1) * C, :] = state
        if r < n - 1:
            kw = flipped(k) * jnp.exp(after[r : r + 1])
            state = jnp.exp(tot[r]) * state + mm(parts(kw, 1), twice(v, 0))


def turned_kernel(q_ref, k_ref, downs_ref, rows_ref, order_ref, scores_ref, upper_ref):
    n = rows_ref.shape[0] // 5
    row = lax.broadcasted_iota(jnp.int32, (C, C), 0)
    col = lax.broadcasted_iota(jnp.int32, (C, C), 1)
    for r in range(n):
        decay = jnp.exp(jnp.minimum(rows_ref[r : r + 1, :] - chunk(downs_ref, r), 0.0))
        upper = jnp.where(row <= col, decay, 0.0)
        upper_ref[r * C : (r + 1) * C, :] = upper
        scores_ref[r * C : (r + 1) * C, :] = parts(mm_nt(chunk(k_ref, r), chunk(q_ref, r)) * upper, 1)


def back_weights(levels, count, payloads):
    own, others = payloads[: len(levels)], payloads[len(levels) :]
    behind = jnp.zeros((1, C), F32)
    weights = []
    at = 0
    for (stride, radix, rounds, back_rounds), own_ref in zip(levels, own, strict=True):
        positions, senders = places(stride, radix, rounds), places(stride, radix, back_rounds)
        mine = positions[0]
        logs = [read_log(ref) for ref in (own_ref, *others[at : at + radix - 1])]
        at += radix - 1
        for position in senders[1:]:
            weight = jnp.exp(behind + between(logs, positions, mine, position))
            weights.append(jnp.where(position > mine, weight, 0.0))
        for position in senders:
            weights.append(jnp.exp(between(logs, positions, -1, position)))
        behind = behind + between(logs, positions, mine, radix)
    weights.append(jnp.zeros((count - len(weights), C), F32))
    return jnp.concatenate(weights, axis=0)


def norm_kernel(levels, local_ref, q_ref, qt_ref, dy_ref, lead_ref, *refs):
    received, (attn_ref, dattn_ref, incoming_ref, state_ref) = refs[:-4], refs[-4:]
    n = local_ref.shape[0] // C
    own, others = received[: len(levels)], received[len(levels) :]
    incoming = jnp.zeros((C, C), F32)
    ahead = jnp.zeros((1, C), F32)
    at = 0
    for (stride, radix, rounds, _), own_ref in zip(levels, own, strict=True):
        positions = places(stride, radix, rounds)
        mine = positions[0]
        level = [own_ref, *others[at : at + radix - 1]]
        at += radix - 1
        logs = [read_log(ref) for ref in level]
        for ref, position in zip(level[1:], positions[1:], strict=True):
            weight = jnp.where(position < mine, jnp.exp(ahead + between(logs, positions, position, mine)), 0.0)
            incoming = incoming + weight * ref[:C, :].astype(F32)
        ahead = ahead + between(logs, positions, -1, mine)
    incoming_ref[...] = incoming
    incoming = incoming.astype(BF16)
    state = jnp.zeros((C, C), F32)
    for r in range(n):
        lead = chunk(lead_ref, r)
        attention = chunk(local_ref, r) + lead * mm(chunk(q_ref, r), incoming)
        dy = chunk(dy_ref, r).astype(F32)
        ratio = lax.rsqrt(jnp.mean(attention * attention, axis=1, keepdims=True) + NORM_EPS)
        along = jnp.sum(dy * attention, axis=1, keepdims=True)
        attn_ref[r * C : (r + 1) * C, :] = (attention * ratio).astype(BF16)
        dattn = ratio * dy - (ratio * ratio * ratio / C * along) * attention
        dattn_ref[r * C : (r + 1) * C, :] = dattn
        state = state + mm(qt_ref[:, r * C : (r + 1) * C], (lead * dattn).astype(BF16))
    state_ref[...] = state.astype(BF16)


def fold_back_kernel(first, radix, own_ref, *refs):
    weights_ref, out_ref = refs[radix - 1], refs[-1]
    total = jnp.zeros((C, C), F32)
    for i, ref in enumerate((own_ref, *refs[: radix - 1])):
        total = total + weights_ref[first + i : first + i + 1, :] * ref[...].astype(F32)
    out_ref[...] = total.astype(BF16)


def queries_kernel(
    levels, count, columns, stride, k_ref, v_ref, downs_ref, rows_ref, starts_ref, lower_ref, dattn_ref, incoming_ref, order_ref, *refs
):
    attn_ref, have_ref, came_ref, *payloads = refs[:-7]
    attn_hbm, dq_hbm, total_hbm, weights_ref, dq_ref, total_ref, sems = refs[-7:]
    n = rows_ref.shape[0] // 5
    copies = [
        pltpu.make_async_copy(source, target, sems.at[i])
        for i, (source, target) in enumerate(((attn_ref, attn_hbm), (total_ref, total_hbm), (dq_ref, dq_hbm)))
    ]
    copies[0].start()
    total_ref[...] = half(have_ref, columns, bit(stride), 0).astype(F32) + came_ref[...].astype(F32)
    copies[1].start()
    incoming = incoming_ref[...]
    for r in range(n):
        pair = parts(chunk(dattn_ref, r), 1)
        dscores = mm_nt(pair, twice(chunk(v_ref, r), 1)) * chunk(lower_ref, r)
        start = chunk(starts_ref, r) + rows_ref[2 * n + r : 2 * n + r + 1, :] * incoming
        dq = mm(parts(dscores, 1), twice(chunk(k_ref, r), 0))
        dq = dq + jnp.exp(chunk(downs_ref, r)) * mm_nt(pair, twice(start.astype(BF16), 1))
        dq_ref[r * C : (r + 1) * C, :] = dq.astype(BF16)
    copies[2].start()
    weights_ref[...] = back_weights(levels, count, payloads)
    for copy in copies:
        copy.wait()


def keys_kernel(
    q_ref, k_ref, v_ref, qt_ref, downs_ref, rows_ref, scores_ref, upper_ref, dattn_ref, order_ref, dk_ref, dv_ref, tail_ref
):
    n = rows_ref.shape[0] // 5
    future = jnp.zeros((C, C), F32)
    for r in reversed(range(n)):
        k, v = chunk(k_ref, r), chunk(v_ref, r)
        dattn = chunk(dattn_ref, r)
        pair = parts(dattn, 1)
        down = chunk(downs_ref, r)
        left = jnp.minimum(rows_ref[3 * n + r : 3 * n + r + 1, :] - down, 0.0)
        tail_ref[r * C : (r + 1) * C, :] = jnp.exp(left + rows_ref[4 * n + r : 4 * n + r + 1, :])
        dscores_t = mm_nt(twice(v, 1), pair) * chunk(upper_ref, r)
        scores = chunk(scores_ref, r)
        dk = mm(parts(dscores_t, 1), twice(chunk(q_ref, r), 0))
        dv = mm(scores, twice(pair[:, :C], 0)) + mm(scores[:, :C], pair[:, C:])
        if r < n - 1:
            tail = jnp.exp(left)
            dk = dk + tail * mm_nt(twice(v, 1), parts(future, 1))
            dv = dv + tail * mm(twice(k, 1), parts(future, 0))
        dk_ref[r * C : (r + 1) * C, :] = dk
        dv_ref[r * C : (r + 1) * C, :] = dv
        if r > 0:
            both = mm(qt_ref[:, r * C : (r + 1) * C], parts(jnp.exp(down) * dattn, 1))
            future = rows_ref[n + r : n + r + 1, :] * future + both[:, :C] + both[:, C:]


def last_kernel(levels, dk_ref, dv_ref, k_ref, v_ref, tail_ref, weights_ref, *refs):
    received, (k_hbm, v_hbm, out_k_ref, out_v_ref, sems) = refs[:-5], refs[-5:]
    n = dk_ref.shape[0] // C
    future = jnp.zeros((C, C), F32)
    at, taken = 0, 0
    for _, radix, _, _ in levels:
        for d in range(radix - 1):
            future = future + weights_ref[at + d : at + d + 1, :] * received[taken + d][...].astype(F32)
        at += 2 * radix - 1
        taken += radix - 1
    future = future.astype(BF16)
    copies = []
    step = 2 * C
    for r in range(n // 2):
        rows = slice(r * step, (r + 1) * step)
        tail = tail_ref[rows, :]
        out_k_ref[rows, :] = (dk_ref[rows, :] + tail * mm_nt(v_ref[rows, :], future)).astype(BF16)
        out_v_ref[rows, :] = (dv_ref[rows, :] + tail * mm(k_ref[rows, :], future)).astype(BF16)
        if (r + 1) % (n // 4) == 0:
            part = pl.ds((r + 1 - n // 4) * step, n // 4 * step)
            for source, target in ((out_k_ref, k_hbm), (out_v_ref, v_hbm)):
                copies.append(pltpu.make_async_copy(source.at[part], target.at[part], sems.at[len(copies)]))
                copies[-1].start()
    for copy in copies:
        copy.wait()


def half(ref, columns, odd, i):
    return ref[:, pl.ds(pl.multiple_of((2 * i + odd) * columns, C), columns)]


def bit(stride):
    return lax.rem(lax.div(lax.axis_index("dp"), stride), 2)


def add_kernel(columns, stride, have_ref, came_ref, kept_ref, sent_ref):
    for i in range(have_ref.shape[1] // columns // 2):
        kept = half(have_ref, columns, bit(stride), i).astype(F32)
        kept_ref[:, i * columns : (i + 1) * columns] = kept + came_ref[:, i * columns : (i + 1) * columns].astype(F32)
    for i in range(kept_ref.shape[1] // columns // 2):
        sent_ref[:, i * columns : (i + 1) * columns] = half(kept_ref, columns, 1 - bit(2 * stride), i).astype(BF16)


def call(body, shapes, name, scratch=(), in_specs=None, out_specs=None, flops=0, moved=1024, vmem=32 << 20):
    specs = {}
    if in_specs is not None:
        specs["in_specs"] = in_specs
    if out_specs is not None:
        specs["out_specs"] = out_specs
    return pl.pallas_call(
        body,
        out_shape=shapes,
        scratch_shapes=scratch,
        name=name,
        compiler_params=pltpu.CompilerParams(vmem_limit_bytes=vmem),
        cost_estimate=pl.CostEstimate(flops=flops, bytes_accessed=moved, transcendentals=0),
        **specs,
    )


def rounds_of(stride, places_to):
    return tuple(
        tuple(targets[at // stride] * stride + at % stride for at in range(stride * len(targets))) for targets in places_to
    )


def scan_levels(size):
    levels, stride = [], 1
    while stride < size:
        radix = 2 if stride == 1 else min(4, size // stride)
        pairs = tuple(tuple(at ^ d for at in range(radix)) for d in range(1, radix))
        forward = rounds_of(stride, FORWARD_OF_4 if radix == 4 else pairs)
        backward = rounds_of(stride, LAST_BACKWARD_OF_4 if radix == 4 and 4 * stride == size else pairs)
        levels.append((stride, radix, forward, backward))
        stride *= radix
    return levels


def send(x, axis, size, targets):
    pairs = [(i, i - i % len(targets) + targets[i % len(targets)]) for i in range(size)]
    return lax.ppermute(x, axis, pairs)


def local(levels, seq, dp, queries, key_vectors, value_vectors, out_grad, log_decay, prev_grads):
    q, k, v, dy = queries[0], key_vectors[0], value_vectors[0], out_grad[0]
    tokens = q.shape[0]
    n = tokens // C
    decay = log_decay.reshape(n, C)
    shape = jax.ShapeDtypeStruct
    payload = shape((C + LOGS, C), BF16)
    square = shape((C, C), F32)
    wide, narrow = shape((tokens, C), F32), shape((tokens, C), BF16)

    away = pl.BlockSpec(memory_space=pltpu.HBM)
    here = pl.BlockSpec(memory_space=pltpu.VMEM)
    whole = pltpu.VMEM((tokens, C), BF16)
    dma = pltpu.SemaphoreType.DMA

    grads = prev_grads[0]
    lines = grads.shape[0]
    columns = grads.shape[1] // dp
    state, sent = call(
        functools.partial(state_kernel, columns),
        (payload, shape((lines, grads.shape[1] // 2), BF16)),
        "state",
        scratch=[whole, whole, pltpu.VMEM((n, C), F32), dma((3 + dp // 2,))],
        in_specs=[away] * 4,
    )(*[pltpu.with_memory_space_constraint(x, pltpu.HBM) for x in (k, v, decay, grads)])
    own = [state]
    others = []
    for i, (stride, radix, rounds, _) in enumerate(levels):
        got = [send(own[-1], "seq", seq, targets) for targets in rounds]
        others += got
        if i == 0:
            came = send(sent, "dp", dp, (1, 0))
            total, part = grads, 1
            while 2 * part < dp:
                kept, sent = shape((lines, total.shape[1] // 2), F32), shape((lines, total.shape[1] // 4), BF16)
                total, sent = call(functools.partial(add_kernel, columns, part), (kept, sent), "add")(total, came)
                part *= 2
                came = send(sent, "dp", dp, rounds_of(part, ((1, 0),))[0])
        if i < len(levels) - 1:
            fold = functools.partial(fold_kernel, stride, radix, rounds)
            own.append(call(fold, payload, "fold")(own[-1], *got, *([total] if i == 0 else [])))
    local_out, downs, rows, qt, starts, lower, lead = call(
        forward_kernel, (wide, wide, shape((5 * n, C), F32), shape((C, tokens), BF16), wide, wide, wide), "forward"
    )(q, k, v, decay, own[-1], dy)
    scores_t, upper = call(turned_kernel, (shape((tokens, 2 * C), BF16), wide), "turned")(q, k, downs, rows, own[-1])
    count = sum(2 * radix - 1 for _, radix, _, _ in levels)
    count += -count % 8
    attention, dattn, incoming, state = call(
        functools.partial(norm_kernel, levels), (narrow, wide, square, shape((C, C), BF16)), "norm"
    )(local_out, q, qt, dy, lead, *own, *others, scores_t)

    attn_out, grad_query, grad_shard, weights = call(
        functools.partial(queries_kernel, levels, count, columns, dp // 2),
        (narrow, narrow, shape((lines, columns), F32), shape((count, C), F32)),
        "queries",
        scratch=[whole, pltpu.VMEM((lines, columns), F32), dma((3,))],
        in_specs=[here] * (12 + len(own) + len(others)),
        out_specs=(away, away, away, here),
    )(k, v, downs, rows, starts, lower, dattn, incoming, state, attention, total, came, *own, *others)
    received = []
    at = 0
    for i, (stride, radix, _, rounds) in enumerate(levels):
        got = [send(state, "seq", seq, targets) for targets in rounds]
        received += got
        if i < len(levels) - 1:
            fold = functools.partial(fold_back_kernel, at + radix - 1, radix)
            state = call(fold, shape((C, C), BF16), "fold_back")(state, *got, weights)
        at += 2 * radix - 1
    dk, dv, tail = call(keys_kernel, (wide, wide, wide), "keys")(q, k, v, qt, downs, rows, scores_t, upper, dattn, state)
    grad_key, grad_value = call(
        functools.partial(last_kernel, levels),
        (narrow, narrow),
        "last",
        scratch=[whole, whole, dma((4,))],
        in_specs=[here] * (6 + len(received)),
        out_specs=(away, away),
    )(dk, dv, k, v, tail, weights, *received)
    return attn_out[None], grad_query[None], grad_key[None], grad_value[None], grad_shard


def solution(mesh):
    seq, dp = mesh.shape["seq"], mesh.shape["dp"]
    return jax.shard_map(
        functools.partial(local, scan_levels(seq), seq, dp),
        mesh=mesh,
        in_specs=(
            P("dp", "seq", None),
            P("dp", "seq", None),
            P("dp", "seq", None),
            P("dp", "seq", None),
            P("dp", None, "seq"),
            P("dp", "seq", None),
        ),
        out_specs=(
            P("dp", "seq", None),
            P("dp", "seq", None),
            P("dp", "seq", None),
            P("dp", "seq", None),
            P("seq", "dp"),
        ),
        check_vma=False,
    )
```

```python
import functools

import jax
import jax.numpy as jnp
from jax import lax
from jax.experimental import pallas as pl
from jax.experimental.pallas import tpu as pltpu
from jax.sharding import PartitionSpec as P

NORM_EPS = 1e-06
C = 128
F32 = jnp.float32
BF16 = jnp.bfloat16
FORWARD_OF_4 = ((3, 0, 1, 2), (2, 3, 0, 1), (1, 2, 3, 0))
LAST_BACKWARD_OF_4 = ((1, 0, 3, 2), (2, 3, 0, 1), (2, 3, 1, 0))
LOGS = 16


def mm(a, b):
    return lax.dot_general(a, b, (((1,), (0,)), ((), ())), preferred_element_type=F32)


def mm_nt(a, b):
    return lax.dot_general(a, b, (((1,), (1,)), ((), ())), preferred_element_type=F32)


def split(x):
    high = x.astype(BF16)
    return high, (x - high.astype(F32)).astype(BF16)


def twice(x, axis):
    return jnp.concatenate([x, x], axis=axis)


def parts(x, axis):
    return jnp.concatenate(split(x), axis=axis)


def cut3(x):
    high = x.astype(BF16).astype(F32)
    middle = (x - high).astype(BF16).astype(F32)
    return high, middle, x - high - middle


def sums(decay):
    n = decay.shape[0]
    row = lax.broadcasted_iota(jnp.int32, (C, C), 0)
    col = lax.broadcasted_iota(jnp.int32, (C, C), 1)
    upto = (row <= col).astype(F32)
    after = (row > col).astype(F32)
    ones = jnp.concatenate([upto, after], axis=1).astype(BF16)
    pieces = jnp.concatenate(cut3(decay), axis=0).astype(BF16)
    both = mm(pieces, ones)
    both = both[:n] + both[n : 2 * n] + both[2 * n :]
    return both[:, :C], both[:, C:]


def totals(upto):
    n = upto.shape[0]
    return [jnp.broadcast_to(upto[r : r + 1, C - 1 :], (1, C)) for r in range(n)]


def before_chunks(tot):
    out = [jnp.zeros((1, C), F32)]
    for t in tot[:-1]:
        out.append(out[-1] + t)
    return out


def after_chunks(tot):
    return before_chunks(tot[::-1])[::-1]


def chunk(ref, r):
    return ref[r * C : (r + 1) * C, :]


def flipped(x):
    return x.astype(F32).T


def log_rows(total):
    high, middle, low = cut3(total)
    return jnp.concatenate([high, middle, low, jnp.zeros((LOGS - 3, C), F32)], axis=0).astype(BF16)


def read_log(ref):
    rows = ref[C:, :].astype(F32)
    return rows[0:1] + rows[1:2] + rows[2:3]


def state_kernel(columns, k_hbm, v_hbm, decay_hbm, grads_hbm, out_ref, sent_ref, k_ref, v_ref, decay_ref, sems):
    pairs = [(decay_hbm, decay_ref), (k_hbm, k_ref), (v_hbm, v_ref)]
    for i in range(grads_hbm.shape[1] // columns // 2):
        block = grads_hbm.at[:, pl.ds(pl.multiple_of((2 * i + 1 - bit(1)) * columns, C), columns)]
        pairs.append((block, sent_ref.at[:, pl.ds(i * columns, columns)]))
    copies = [pltpu.make_async_copy(source, target, sems.at[i]) for i, (source, target) in enumerate(pairs)]
    for copy in copies:
        copy.start()
    copies[0].wait()
    upto, after = sums(decay_ref[...])
    tot = totals(upto)
    later = after_chunks(tot)
    weights = [jnp.exp(after[r : r + 1] + later[r]) for r in range(len(tot))]
    copies[1].wait()
    copies[2].wait()
    state = jnp.zeros((C, C), F32)
    for r in range(0, len(weights), 2):
        kw = [(flipped(chunk(k_ref, i)) * weights[i]).astype(BF16) for i in (r, r + 1)]
        state = state + mm(jnp.concatenate(kw, axis=1), v_ref[r * C : (r + 2) * C, :])
    out_ref[:C, :] = state.astype(BF16)
    out_ref[C:, :] = log_rows(sum(tot))
    for copy in copies[3:]:
        copy.wait()


def between(logs, positions, low, high):
    out = jnp.zeros((1, C), F32)
    for log, position in zip(logs, positions, strict=True):
        out = out + jnp.where((position > low) & (position < high), log, 0.0)
    return out


def places(stride, radix, rounds):
    block = lax.rem(lax.axis_index("seq"), stride * radix)
    senders = [sum(jnp.where(block == to, at // stride, 0) for at, to in enumerate(targets)) for targets in rounds]
    return [lax.div(block, stride), *senders]


def fold_kernel(stride, radix, rounds, own_ref, *refs):
    out_ref = refs[-1]
    positions = places(stride, radix, rounds)
    all_refs = [own_ref, *refs[: radix - 1]]
    logs = [read_log(ref) for ref in all_refs]
    total = jnp.zeros((C, C), F32)
    for ref, position in zip(all_refs, positions, strict=True):
        weight = jnp.exp(between(logs, positions, position, radix))
        total = total + weight * ref[:C, :].astype(F32)
    out_ref[:C, :] = total.astype(BF16)
    out_ref[C:, :] = log_rows(sum(logs))


def spread(decay_row):
    row = lax.broadcasted_iota(jnp.int32, (C, C), 0)
    col = lax.broadcasted_iota(jnp.int32, (C, C), 1)
    pieces = jnp.concatenate([jnp.where(row >= col, x, 0.0) for x in cut3(decay_row)], axis=1).astype(BF16)
    return mm(pieces, jnp.ones((3 * C, C), BF16))


def forward_kernel(
    q_ref, k_ref, v_ref, decay_ref, order_ref, dy_ref, out_ref, downs_ref, rows_ref, qt_ref, starts_ref, lower_ref, lead_ref
):
    upto, after = sums(decay_ref[...])
    tot = totals(upto)
    begin, later = before_chunks(tot), after_chunks(tot)
    n = len(tot)
    row = lax.broadcasted_iota(jnp.int32, (C, C), 0)
    col = lax.broadcasted_iota(jnp.int32, (C, C), 1)
    rows_ref[:n, :] = upto
    for i, rows in enumerate(([jnp.exp(x) for x in tot], [jnp.exp(x) for x in begin], tot, later), 1):
        rows_ref[i * n : (i + 1) * n, :] = jnp.concatenate(rows, axis=0)
    state = jnp.zeros((C, C), F32)
    for r in range(n):
        q, k, v = chunk(q_ref, r), chunk(k_ref, r), chunk(v_ref, r)
        down = spread(decay_ref[r : r + 1, :])
        downs_ref[r * C : (r + 1) * C, :] = down
        lead_ref[r * C : (r + 1) * C, :] = jnp.exp(down + begin[r])
        lower = jnp.where(row >= col, jnp.exp(jnp.minimum(down - upto[r : r + 1], 0.0)), 0.0)
        lower_ref[r * C : (r + 1) * C, :] = lower
        scores = mm_nt(q, k) * lower
        out = mm(parts(scores, 1), twice(v, 0))
        if r > 0:
            out = out + jnp.exp(down) * mm(twice(q, 1), parts(state, 0))
        out_ref[r * C : (r + 1) * C, :] = out
        qt_ref[:, r * C : (r + 1) * C] = flipped(q).astype(BF16)
        starts_ref[r * C : (r + 1) * C, :] = state
        if r < n - 1:
            kw = flipped(k) * jnp.exp(after[r : r + 1])
            state = jnp.exp(tot[r]) * state + mm(parts(kw, 1), twice(v, 0))


def turned_kernel(q_ref, k_ref, downs_ref, rows_ref, order_ref, scores_ref, upper_ref):
    n = rows_ref.shape[0] // 5
    row = lax.broadcasted_iota(jnp.int32, (C, C), 0)
    col = lax.broadcasted_iota(jnp.int32, (C, C), 1)
    for r in range(n):
        decay = jnp.exp(jnp.minimum(rows_ref[r : r + 1, :] - chunk(downs_ref, r), 0.0))
        upper = jnp.where(row <= col, decay, 0.0)
        upper_ref[r * C : (r + 1) * C, :] = upper
        scores_ref[r * C : (r + 1) * C, :] = parts(mm_nt(chunk(k_ref, r), chunk(q_ref, r)) * upper, 1)


def back_weights(levels, count, payloads):
    own, others = payloads[: len(levels)], payloads[len(levels) :]
    behind = jnp.zeros((1, C), F32)
    weights = []
    at = 0
    for (stride, radix, rounds, back_rounds), own_ref in zip(levels, own, strict=True):
        positions, senders = places(stride, radix, rounds), places(stride, radix, back_rounds)
        mine = positions[0]
        logs = [read_log(ref) for ref in (own_ref, *others[at : at + radix - 1])]
        at += radix - 1
        for position in senders[1:]:
            weight = jnp.exp(behind + between(logs, positions, mine, position))
            weights.append(jnp.where(position > mine, weight, 0.0))
        for position in senders:
            weights.append(jnp.exp(between(logs, positions, -1, position)))
        behind = behind + between(logs, positions, mine, radix)
    weights.append(jnp.zeros((count - len(weights), C), F32))
    return jnp.concatenate(weights, axis=0)


def norm_kernel(levels, local_ref, q_ref, qt_ref, dy_ref, lead_ref, *refs):
    received, (attn_ref, dattn_ref, incoming_ref, state_ref) = refs[:-4], refs[-4:]
    n = local_ref.shape[0] // C
    own, others = received[: len(levels)], received[len(levels) :]
    incoming = jnp.zeros((C, C), F32)
    ahead = jnp.zeros((1, C), F32)
    at = 0
    for (stride, radix, rounds, _), own_ref in zip(levels, own, strict=True):
        positions = places(stride, radix, rounds)
        mine = positions[0]
        level = [own_ref, *others[at : at + radix - 1]]
        at += radix - 1
        logs = [read_log(ref) for ref in level]
        for ref, position in zip(level[1:], positions[1:], strict=True):
            weight = jnp.where(position < mine, jnp.exp(ahead + between(logs, positions, position, mine)), 0.0)
            incoming = incoming + weight * ref[:C, :].astype(F32)
        ahead = ahead + between(logs, positions, -1, mine)
    incoming_ref[...] = incoming
    incoming = incoming.astype(BF16)
    state = jnp.zeros((C, C), F32)
    for r in range(n):
        lead = chunk(lead_ref, r)
        attention = chunk(local_ref, r) + lead * mm(chunk(q_ref, r), incoming)
        dy = chunk(dy_ref, r).astype(F32)
        ratio = lax.rsqrt(jnp.mean(attention * attention, axis=1, keepdims=True) + NORM_EPS)
        along = jnp.sum(dy * attention, axis=1, keepdims=True)
        attn_ref[r * C : (r + 1) * C, :] = (attention * ratio).astype(BF16)
        dattn = ratio * dy - (ratio * ratio * ratio / C * along) * attention
        dattn_ref[r * C : (r + 1) * C, :] = dattn
        state = state + mm(qt_ref[:, r * C : (r + 1) * C], (lead * dattn).astype(BF16))
    state_ref[...] = state.astype(BF16)


def fold_back_kernel(first, radix, own_ref, *refs):
    weights_ref, out_ref = refs[radix - 1], refs[-1]
    total = jnp.zeros((C, C), F32)
    for i, ref in enumerate((own_ref, *refs[: radix - 1])):
        total = total + weights_ref[first + i : first + i + 1, :] * ref[...].astype(F32)
    out_ref[...] = total.astype(BF16)


def queries_kernel(
    levels, count, columns, stride, k_ref, v_ref, downs_ref, rows_ref, starts_ref, lower_ref, dattn_ref, incoming_ref, order_ref, *refs
):
    attn_ref, have_ref, came_ref, *payloads = refs[:-7]
    attn_hbm, dq_hbm, total_hbm, weights_ref, dq_ref, total_ref, sems = refs[-7:]
    n = rows_ref.shape[0] // 5
    copies = [
        pltpu.make_async_copy(source, target, sems.at[i])
        for i, (source, target) in enumerate(((attn_ref, attn_hbm), (total_ref, total_hbm), (dq_ref, dq_hbm)))
    ]
    copies[0].start()
    total_ref[...] = half(have_ref, columns, bit(stride), 0).astype(F32) + came_ref[...].astype(F32)
    copies[1].start()
    incoming = incoming_ref[...]
    for r in range(n):
        pair = parts(chunk(dattn_ref, r), 1)
        dscores = mm_nt(pair, twice(chunk(v_ref, r), 1)) * chunk(lower_ref, r)
        start = chunk(starts_ref, r) + rows_ref[2 * n + r : 2 * n + r + 1, :] * incoming
        dq = mm(parts(dscores, 1), twice(chunk(k_ref, r), 0))
        dq = dq + jnp.exp(chunk(downs_ref, r)) * mm_nt(pair, twice(start.astype(BF16), 1))
        dq_ref[r * C : (r + 1) * C, :] = dq.astype(BF16)
    copies[2].start()
    weights_ref[...] = back_weights(levels, count, payloads)
    for copy in copies:
        copy.wait()


def keys_kernel(
    q_ref, k_ref, v_ref, qt_ref, downs_ref, rows_ref, scores_ref, upper_ref, dattn_ref, order_ref, dk_ref, dv_ref, kt_ref, vt_ref
):
    n = rows_ref.shape[0] // 5
    future = jnp.zeros((C, C), F32)
    for r in reversed(range(n)):
        k, v = chunk(k_ref, r), chunk(v_ref, r)
        dattn = chunk(dattn_ref, r)
        pair = parts(dattn, 1)
        down = chunk(downs_ref, r)
        left = jnp.minimum(rows_ref[3 * n + r : 3 * n + r + 1, :] - down, 0.0)
        whole_tail = jnp.exp(left + rows_ref[4 * n + r : 4 * n + r + 1, :])
        kt_ref[r * C : (r + 1) * C, :] = (whole_tail * k.astype(F32)).astype(BF16)
        vt_ref[r * C : (r + 1) * C, :] = (whole_tail * v.astype(F32)).astype(BF16)
        dscores_t = mm_nt(twice(v, 1), pair) * chunk(upper_ref, r)
        scores = chunk(scores_ref, r)
        dk = mm(parts(dscores_t, 1), twice(chunk(q_ref, r), 0))
        dv = mm(scores, twice(pair[:, :C], 0)) + mm(scores[:, :C], pair[:, C:])
        if r < n - 1:
            tail = jnp.exp(left)
            dk = dk + tail * mm_nt(twice(v, 1), parts(future, 1))
            dv = dv + tail * mm(twice(k, 1), parts(future, 0))
        dk_ref[r * C : (r + 1) * C, :] = dk
        dv_ref[r * C : (r + 1) * C, :] = dv
        if r > 0:
            both = mm(qt_ref[:, r * C : (r + 1) * C], parts(jnp.exp(down) * dattn, 1))
            future = rows_ref[n + r : n + r + 1, :] * future + both[:, :C] + both[:, C:]


def last_kernel(levels, dk_ref, dv_ref, kt_ref, vt_ref, weights_ref, *refs):
    received, (k_hbm, v_hbm, out_k_ref, out_v_ref, sems) = refs[:-5], refs[-5:]
    n = dk_ref.shape[0] // C
    future = jnp.zeros((C, C), F32)
    at, taken = 0, 0
    for _, radix, _, _ in levels:
        for d in range(radix - 1):
            future = future + weights_ref[at + d : at + d + 1, :] * received[taken + d][...].astype(F32)
        at += 2 * radix - 1
        taken += radix - 1
    future = future.astype(BF16)
    copies = []
    step = 2 * C
    for r in range(n // 2):
        rows = slice(r * step, (r + 1) * step)
        out_k_ref[rows, :] = (dk_ref[rows, :] + mm_nt(vt_ref[rows, :], future)).astype(BF16)
        out_v_ref[rows, :] = (dv_ref[rows, :] + mm(kt_ref[rows, :], future)).astype(BF16)
        if (r + 1) % (n // 4) == 0:
            part = pl.ds((r + 1 - n // 4) * step, n // 4 * step)
            for source, target in ((out_k_ref, k_hbm), (out_v_ref, v_hbm)):
                copies.append(pltpu.make_async_copy(source.at[part], target.at[part], sems.at[len(copies)]))
                copies[-1].start()
    for copy in copies:
        copy.wait()


def half(ref, columns, odd, i):
    return ref[:, pl.ds(pl.multiple_of((2 * i + odd) * columns, C), columns)]


def bit(stride):
    return lax.rem(lax.div(lax.axis_index("dp"), stride), 2)


def add_kernel(columns, stride, have_ref, came_ref, kept_ref, sent_ref):
    for i in range(have_ref.shape[1] // columns // 2):
        kept = half(have_ref, columns, bit(stride), i).astype(F32)
        kept_ref[:, i * columns : (i + 1) * columns] = kept + came_ref[:, i * columns : (i + 1) * columns].astype(F32)
    for i in range(kept_ref.shape[1] // columns // 2):
        sent_ref[:, i * columns : (i + 1) * columns] = half(kept_ref, columns, 1 - bit(2 * stride), i).astype(BF16)


def call(body, shapes, name, scratch=(), in_specs=None, out_specs=None, flops=0, moved=1024, vmem=32 << 20):
    specs = {}
    if in_specs is not None:
        specs["in_specs"] = in_specs
    if out_specs is not None:
        specs["out_specs"] = out_specs
    return pl.pallas_call(
        body,
        out_shape=shapes,
        scratch_shapes=scratch,
        name=name,
        compiler_params=pltpu.CompilerParams(vmem_limit_bytes=vmem),
        cost_estimate=pl.CostEstimate(flops=flops, bytes_accessed=moved, transcendentals=0),
        **specs,
    )


def rounds_of(stride, places_to):
    return tuple(
        tuple(targets[at // stride] * stride + at % stride for at in range(stride * len(targets))) for targets in places_to
    )


def scan_levels(size):
    levels, stride = [], 1
    while stride < size:
        radix = 2 if stride == 1 else min(4, size // stride)
        pairs = tuple(tuple(at ^ d for at in range(radix)) for d in range(1, radix))
        forward = rounds_of(stride, FORWARD_OF_4 if radix == 4 else pairs)
        backward = rounds_of(stride, LAST_BACKWARD_OF_4 if radix == 4 and 4 * stride == size else pairs)
        levels.append((stride, radix, forward, backward))
        stride *= radix
    return levels


def send(x, axis, size, targets):
    pairs = [(i, i - i % len(targets) + targets[i % len(targets)]) for i in range(size)]
    return lax.ppermute(x, axis, pairs)


def local(levels, seq, dp, queries, key_vectors, value_vectors, out_grad, log_decay, prev_grads):
    q, k, v, dy = queries[0], key_vectors[0], value_vectors[0], out_grad[0]
    tokens = q.shape[0]
    n = tokens // C
    decay = log_decay.reshape(n, C)
    shape = jax.ShapeDtypeStruct
    payload = shape((C + LOGS, C), BF16)
    square = shape((C, C), F32)
    wide, narrow = shape((tokens, C), F32), shape((tokens, C), BF16)

    away = pl.BlockSpec(memory_space=pltpu.HBM)
    here = pl.BlockSpec(memory_space=pltpu.VMEM)
    whole = pltpu.VMEM((tokens, C), BF16)
    dma = pltpu.SemaphoreType.DMA

    grads = prev_grads[0]
    lines = grads.shape[0]
    columns = grads.shape[1] // dp
    state, sent = call(
        functools.partial(state_kernel, columns),
        (payload, shape((lines, grads.shape[1] // 2), BF16)),
        "state",
        scratch=[whole, whole, pltpu.VMEM((n, C), F32), dma((3 + dp // 2,))],
        in_specs=[away] * 4,
    )(*[pltpu.with_memory_space_constraint(x, pltpu.HBM) for x in (k, v, decay, grads)])
    own = [state]
    others = []
    for i, (stride, radix, rounds, _) in enumerate(levels):
        got = [send(own[-1], "seq", seq, targets) for targets in rounds]
        others += got
        if i == 0:
            came = send(sent, "dp", dp, (1, 0))
            total, part = grads, 1
            while 2 * part < dp:
                kept, sent = shape((lines, total.shape[1] // 2), F32), shape((lines, total.shape[1] // 4), BF16)
                total, sent = call(functools.partial(add_kernel, columns, part), (kept, sent), "add")(total, came)
                part *= 2
                came = send(sent, "dp", dp, rounds_of(part, ((1, 0),))[0])
        if i < len(levels) - 1:
            fold = functools.partial(fold_kernel, stride, radix, rounds)
            own.append(call(fold, payload, "fold")(own[-1], *got, *([total] if i == 0 else [])))
    local_out, downs, rows, qt, starts, lower, lead = call(
        forward_kernel, (wide, wide, shape((5 * n, C), F32), shape((C, tokens), BF16), wide, wide, wide), "forward"
    )(q, k, v, decay, own[-1], dy)
    scores_t, upper = call(turned_kernel, (shape((tokens, 2 * C), BF16), wide), "turned")(q, k, downs, rows, own[-1])
    count = sum(2 * radix - 1 for _, radix, _, _ in levels)
    count += -count % 8
    attention, dattn, incoming, state = call(
        functools.partial(norm_kernel, levels), (narrow, wide, square, shape((C, C), BF16)), "norm"
    )(local_out, q, qt, dy, lead, *own, *others, scores_t)

    attn_out, grad_query, grad_shard, weights = call(
        functools.partial(queries_kernel, levels, count, columns, dp // 2),
        (narrow, narrow, shape((lines, columns), F32), shape((count, C), F32)),
        "queries",
        scratch=[whole, pltpu.VMEM((lines, columns), F32), dma((3,))],
        in_specs=[here] * (12 + len(own) + len(others)),
        out_specs=(away, away, away, here),
    )(k, v, downs, rows, starts, lower, dattn, incoming, state, attention, total, came, *own, *others)
    received = []
    at = 0
    for i, (stride, radix, _, rounds) in enumerate(levels):
        got = [send(state, "seq", seq, targets) for targets in rounds]
        received += got
        if i < len(levels) - 1:
            fold = functools.partial(fold_back_kernel, at + radix - 1, radix)
            state = call(fold, shape((C, C), BF16), "fold_back")(state, *got, weights)
        at += 2 * radix - 1
    dk, dv, kt, vt = call(keys_kernel, (wide, wide, narrow, narrow), "keys")(q, k, v, qt, downs, rows, scores_t, upper, dattn, state)
    grad_key, grad_value = call(
        functools.partial(last_kernel, levels),
        (narrow, narrow),
        "last",
        scratch=[whole, whole, dma((4,))],
        in_specs=[here] * (5 + len(received)),
        out_specs=(away, away),
    )(dk, dv, kt, vt, weights, *received)
    return attn_out[None], grad_query[None], grad_key[None], grad_value[None], grad_shard


def solution(mesh):
    seq, dp = mesh.shape["seq"], mesh.shape["dp"]
    return jax.shard_map(
        functools.partial(local, scan_levels(seq), seq, dp),
        mesh=mesh,
        in_specs=(
            P("dp", "seq", None),
            P("dp", "seq", None),
            P("dp", "seq", None),
            P("dp", "seq", None),
            P("dp", None, "seq"),
            P("dp", "seq", None),
        ),
        out_specs=(
            P("dp", "seq", None),
            P("dp", "seq", None),
            P("dp", "seq", None),
            P("dp", "seq", None),
            P("seq", "dp"),
        ),
        check_vma=False,
    )
```
